32 devices in a mesh: freq: 2 (over y), gx: 4 (over z), gy: 2 (over x), col: 2 (over core).
Axes of the slice: x: 2, y: 2, z: 4, core: 2. Of those that a mesh axis runs over, the one named last changes fastest.
Arguments:
- source: bfloat16 [12, 64, 32, 256], P('freq', 'gx', 'gy', 'col'), parts along dimension 0, may hold values from -6 to 6
- warm: bfloat16 [12, 64, 32, 256], P('freq', 'gx', 'gy', 'col'), parts along dimension 0, may hold values from -2.1 to 2.6
- forward: bfloat16 [12, 64, 32, 256], P('freq', 'gx', 'gy', 'col'), parts along dimension 0, may hold values from -6 to 6
- density: bfloat16 [64, 32, 256], P('gx', 'gy', 'col'), may hold values from 1 to 3
- material_map: int32 [8, 4, 8], P('gx', 'gy', 'col'), may hold values from 0 to 7
- material_table: float32 [8, 2], replicated, may hold values from 0.5 to 2
- iface_cells: int32 [16, 256], P(('gx', 'gy', 'col')), may hold values from 0 to 32767, as said below
- impedance: float32 [2, 3], replicated, may hold values from 2 to 8
- omega2: float32 [2], P('freq'), parts along dimension 0, may hold values from 0.5 to 1
Outputs:
- adjoint: float32 [12, 64, 32, 256], P('freq', 'gx', 'gy', 'col'), parts along dimension 0
- coarse_gradient: float32 [32, 8], P('freq'), parts along dimension 0
The draws below stay inside these ranges and needn't reach their ends.
There are 2 independent parts, one for each index of `freq`. The reference program is written for one: setup_inputs(seed, part) draws one part's arguments, and reference() takes and returns one part's arrays. A program takes and returns all parts, laid end to end along the dimension named above; an argument that names none is the same for every part. Nothing has to cross between parts.
Inputs may be any that keep to these rules, and one draw needn't show every extreme that they name: `iface_cells`: each row's entries are distinct, rising, and within the tile of 16 x 16 x 128 cells; row r belongs to the device of that index along gx, gy and col together.
All inputs are finite; a program needn't handle non-finite values.
Results may differ from the reference program's by a relative error of at most 0.0003.
Values may be sent and summed in bfloat16 or wider, within the bound.
A program may use at most 64 MiB of HBM per device.

```python
import math
import jax
import jax.numpy as jnp
from jax import lax

CX = 16
CY = 16
CZ = 128
IFC = 256
NMAT = 8
GROUP = 16
NX = 64
NY = 32
NZ = 256
N_GX = 4
N_GY = 2
N_COL = 2


def draw_warm(key, part):
    noise = jnp.clip(0.4 * jax.random.normal(jax.random.fold_in(key, 11), (6, NX, NY, NZ), jnp.float32), -1.6, 1.6)
    tiles_x = NX // CX
    tiles_y = NY // CY
    tiles_z = NZ // CZ
    levels = jax.random.uniform(jax.random.fold_in(key, 12), (6, tiles_x, tiles_y, tiles_z), jnp.float32, -0.5, 1.0)
    spread = jnp.broadcast_to(levels[:, :, None, :, None, :, None], (6, tiles_x, CX, tiles_y, CY, tiles_z, CZ))
    drift = spread.reshape(6, NX, NY, NZ)
    return (noise + drift).astype(jnp.bfloat16)


def draw_iface_cells(key, part):
    stride = CX * CY * CZ // IFC
    offsets = jax.random.randint(jax.random.fold_in(key, 21), (GROUP, IFC), 0, stride)
    row_index = lax.broadcasted_iota(jnp.int32, (GROUP, IFC), 0)
    col_index = lax.broadcasted_iota(jnp.int32, (GROUP, IFC), 1)
    offsets = jnp.where((row_index == 0) & (col_index == 0), 0, offsets)
    offsets = jnp.where((row_index == GROUP - 1) & (col_index == IFC - 1), stride - 1, offsets)
    return (col_index * stride + offsets).astype(jnp.int32)


def plant(drawn, stream_key, smallest, high):
    longest = drawn.shape.index(max(drawn.shape))
    spots = []
    for shift in (0, 1):
        where = [jax.random.randint(jax.random.fold_in(stream_key, axis), (), 0, length) for axis, length in enumerate(drawn.shape)]
        where[longest] = (where[longest] + shift) % drawn.shape[longest]
        spots.append(tuple(where))
    return drawn.at[spots[0]].set(smallest).at[spots[1]].set(high)


def steps_of(stream_key, shape, shards, least, largest):
    level = 1.0
    for dim, shards_of in shards:
        draws = jax.random.uniform(jax.random.fold_in(jax.random.fold_in(stream_key, 6), dim), (shards_of,), jnp.float32, least / len(shards), largest / len(shards))
        level = level * jnp.repeat(jnp.exp(draws), shape[dim] // shards_of).reshape((-1,) + (1,) * (len(shape) - 1 - dim))
    return level


def gaussian(own_key, dims, scale, limit, shards=(), held_as=jnp.bfloat16):
    level = steps_of(own_key, dims, shards, -0.22, 0.18) if shards else 1.0
    array = jax.random.normal(own_key, dims, jnp.float32) * scale * level
    return jnp.minimum(jnp.maximum(array, -limit), limit).astype(held_as)


def setup_inputs(seed: int = 0, part: int = 0) -> dict:
    keys = jax.random.split(jax.random.key(seed), 10)
    part_keys = jax.random.split(jax.random.fold_in(keys[9], part), 10)
    return {
        "source": gaussian(part_keys[0], (6, NX, NY, NZ), 1.0, 6.0, ((1, 4), (2, 2), (3, 2))),
        "warm": draw_warm(jax.random.fold_in(jax.random.fold_in(keys[9], part), 71), part),
        "forward": gaussian(part_keys[2], (6, NX, NY, NZ), 1.0, 6.0, ((1, 4), (2, 2), (3, 2))),
        "density": jnp.clip(jnp.exp(math.log(3.0) - 1.0986123 * jax.random.uniform(keys[3], (NX, NY, NZ), jnp.float32) ** steps_of(keys[3], (NX, NY, NZ), ((0, 4), (1, 2), (2, 2)), -0.2, 0.2)), 1.0, 3.0).astype(jnp.bfloat16),
        "material_map": plant(jax.random.randint(keys[4], (NX // 8, NY // 8, NZ // 32), 0, NMAT), jax.random.fold_in(keys[4], 1), 0, NMAT - 1).astype(jnp.int32),
        "material_table": jnp.clip(jnp.exp(jax.random.uniform(keys[5], (NMAT, 2), jnp.float32, math.log(0.5), math.log(2.0))), 0.5, 2.0),
        "iface_cells": draw_iface_cells(jax.random.fold_in(keys[9], 71), part),
        "impedance": jnp.clip(jnp.exp(jax.random.uniform(keys[7], (2, 3), jnp.float32, math.log(2.0), math.log(8.0))), 2.0, 8.0),
        "omega2": jnp.clip(jax.random.uniform(part_keys[8], (1,), jnp.float32, 0.5, 1.0), 0.5, 1.0),
    }


DAMPING = 0.5
RELAXATION = 0.6


def window(padded, offset):
    size_x = padded.shape[1] - 2
    size_y = padded.shape[2] - 2
    size_z = padded.shape[3] - 2
    return padded[:, 1 + offset[0]:1 + offset[0] + size_x, 1 + offset[1]:1 + offset[1] + size_y, 1 + offset[2]:1 + offset[2] + size_z]


def navier(padded, lame_first, shear):
    units = ((1, 0, 0), (0, 1, 0), (0, 0, 1))
    centre = window(padded, (0, 0, 0))
    second = []
    for axis_d in range(3):
        ahead = units[axis_d]
        behind = tuple(-value for value in ahead)
        second.append(window(padded, ahead) + window(padded, behind) - 2.0 * centre)
    laplace = second[0] + second[1] + second[2]
    result = []
    for part_index in range(2):
        for component in range(3):
            channel = part_index * 3 + component
            divergence = second[component][channel]
            for other_axis in range(3):
                if other_axis != component:
                    source_channel = part_index * 3 + other_axis
                    single = padded[source_channel:source_channel + 1]
                    first_unit = units[component]
                    other_unit = units[other_axis]
                    plus_plus = tuple(first_unit[k] + other_unit[k] for k in range(3))
                    plus_minus = tuple(first_unit[k] - other_unit[k] for k in range(3))
                    minus_plus = tuple(-first_unit[k] + other_unit[k] for k in range(3))
                    minus_minus = tuple(-first_unit[k] - other_unit[k] for k in range(3))
                    mixed = window(single, plus_plus) - window(single, plus_minus) - window(single, minus_plus) + window(single, minus_minus)
                    divergence = divergence + 0.25 * mixed[0]
            result.append(shear * laplace[channel] + (lame_first + shear) * divergence)
    return jnp.stack(result)


def sweep(padded, lame_first, shear, density, mask, source, mean_field, omega_sq, impedance):
    field = window(padded, (0, 0, 0))
    elastic = navier(padded, lame_first, shear)
    real_part = field[:3]
    imag_part = field[3:]
    mean_real = mean_field[:3][:, None, None, None]
    mean_imag = mean_field[3:][:, None, None, None]
    imp_real = impedance[0][:, None, None, None]
    imp_imag = impedance[1][:, None, None, None]
    inertia = omega_sq * density
    diff_real = real_part - mean_real
    diff_imag = imag_part - mean_imag
    apply_real = -elastic[:3] - inertia * (real_part - DAMPING * imag_part) + mask * (imp_real * diff_real - imp_imag * diff_imag)
    apply_imag = -elastic[3:] - inertia * (imag_part + DAMPING * real_part) + mask * (imp_real * diff_imag + imp_imag * diff_real)
    resid_real = source[:3] - apply_real
    resid_imag = source[3:] - apply_imag
    diag_real = 8.0 * shear + 2.0 * lame_first - inertia + mask * imp_real
    diag_imag = -DAMPING * inertia + mask * imp_imag
    modulus = diag_real * diag_real + diag_imag * diag_imag
    new_real = real_part + RELAXATION * (resid_real * diag_real + resid_imag * diag_imag) / modulus
    new_imag = imag_part + RELAXATION * (resid_imag * diag_real - resid_real * diag_imag) / modulus
    return jnp.concatenate([new_real, new_imag], 0)


def expand(blocks):
    blocks_x, blocks_y, blocks_z = blocks.shape
    spread = jnp.broadcast_to(blocks[:, None, :, None, :, None], (blocks_x, 8, blocks_y, 8, blocks_z, 32))
    return spread.reshape(blocks_x * 8, blocks_y * 8, blocks_z * 32)


def material(block_ids, table):
    lame_first = jnp.zeros(block_ids.shape, jnp.float32)
    shear = jnp.zeros(block_ids.shape, jnp.float32)
    for entry in range(table.shape[0]):
        chosen = block_ids == entry
        lame_first = jnp.where(chosen, table[entry, 0], lame_first)
        shear = jnp.where(chosen, table[entry, 1], shear)
    return lame_first, shear


def reference(source, warm, forward, density, material_map, material_table, iface_cells, impedance, omega2):
    omega_sq = omega2[0]
    lame_first, shear = material(expand(material_map), material_table)
    density_cells = density.astype(jnp.float32)
    tile_cells = CX * CY * CZ

    def tile_mask(positions):
        return jnp.zeros((tile_cells,), jnp.float32).at[positions].set(1.0)

    local_masks = jax.vmap(tile_mask)(iface_cells)
    mask = local_masks.reshape(N_GX, N_GY, N_COL, CX, CY, CZ).transpose(0, 3, 1, 4, 2, 5).reshape(NX, NY, NZ)
    count = jnp.float32(GROUP * IFC)
    source_cells = source.astype(jnp.float32)
    field = warm.astype(jnp.float32)
    for sweep_index in range(2):
        mean_field = jnp.sum(mask * field, axis=(1, 2, 3)) / count
        padded = jnp.pad(field, ((0, 0), (1, 1), (1, 1), (1, 1)))
        field = sweep(padded, lame_first, shear, density_cells, mask, source_cells, mean_field, omega_sq, impedance)
    forward_cells = forward.astype(jnp.float32)
    correlation = (field[:3] * forward_cells[:3] - field[3:] * forward_cells[3:]) - DAMPING * (field[:3] * forward_cells[3:] + field[3:] * forward_cells[:3])
    cell_terms = -omega_sq * jnp.sum(correlation, axis=0)
    coarse = cell_terms.reshape(NX // 4, 4, NY // 4, 4, NZ).sum(axis=(1, 3, 4)) / 64.0
    return field, coarse
```

```python
import functools
import jax
import jax.numpy as jnp
from jax import lax
from jax.experimental import pallas as pl
from jax.experimental.pallas import tpu as pltpu
from jax.sharding import PartitionSpec as P

DAMPING = 0.5
RELAXATION = 0.6
MESH_ID = pl.DeviceIdType.MESH
TOP = 8


def kernel(
    n_gx, n_gy, n_col,
    warm_ref, source_hbm, density_hbm, forward_hbm, cells_ref,
    map_ref, table_ref, imp_ref, omega_ref,
    out_hbm, coarse_ref,
    f0, f1, zbuf0, zbuf1, zsend0, zsend1, sums0, sums1, sums2, msg0, msg1, msg2,
    mask_s, mu_s, lm_s, dinv, source_s, density_s, forward_s, out_s,
    local_sem, halo_send, halo_recv, sum_send, sum_recv,
):
    f32 = jnp.float32
    cx, cy, cz = warm_ref.shape[1:]
    cells = cells_ref.shape[1]
    group = n_gx * n_gy * n_col
    gx = lax.axis_index("gx")
    gy = lax.axis_index("gy")
    col = lax.axis_index("col")
    me = (gx * n_gy + gy) * n_col + col

    def coords(index):
        return {"gx": index // (n_gy * n_col), "gy": index // n_col % n_gy, "col": index % n_col}

    def peer(p):
        return lax.rem(me + p, group)

    barrier = pltpu.get_barrier_semaphore()
    for p in range(1, group):
        pl.semaphore_signal(barrier, inc=1, device_id=coords(peer(p)), device_id_type=MESH_ID)

    load_density = pltpu.make_async_copy(density_hbm, density_s, local_sem.at[0])
    load_source = pltpu.make_async_copy(source_hbm, source_s, local_sem.at[1])
    load_forward = pltpu.make_async_copy(forward_hbm, forward_s, local_sem.at[2])
    load_density.start()
    load_source.start()
    load_forward.start()

    lane = lax.broadcasted_iota(jnp.int32, (cy, cz), 1)
    row = lax.broadcasted_iota(jnp.int32, (cy, cz), 0)
    lane1 = lax.broadcasted_iota(jnp.int32, (1, cz), 1)
    edge = jnp.where(col == 0, cz - 1, 0)
    omega = omega_ref[0]

    idx = cells_ref[...]
    hot_row = jnp.where(
        lax.broadcasted_iota(jnp.int32, (cx * cy, cells), 0) == idx // cz, 1.0, 0.0
    ).astype(jnp.bfloat16)
    hot_lane = jnp.where(
        lax.broadcasted_iota(jnp.int32, (cz, cells), 0) == idx % cz, 1.0, 0.0
    ).astype(jnp.bfloat16)
    mask = lax.dot_general(
        hot_row, hot_lane, (((1,), (1,)), ((), ())), preferred_element_type=f32
    )
    mask_s[...] = mask.reshape(cx, cy, cz)

    blocks = map_ref.shape
    for bx in range(blocks[0]):
        mus = []
        lms = []
        for by in range(blocks[1]):
            mu = jnp.zeros((8, cz), f32)
            lm = jnp.zeros((8, cz), f32)
            for bz in range(blocks[2]):
                entry = map_ref[bx, by, bz]
                here = lane[:8] // 32 == bz
                lm = jnp.where(here, table_ref[entry, 0], lm)
                mu = jnp.where(here, table_ref[entry, 1], mu)
            mus.append(mu)
            lms.append(lm + mu)
        mu_s[bx] = jnp.concatenate(mus, 0)
        lm_s[bx] = jnp.concatenate(lms, 0)
    mu_edge = jnp.zeros((cy, cz), f32)
    lm_edge = jnp.zeros((cy, cz), f32)
    edge_block = jnp.where(col == 0, blocks[2] - 1, 0)
    for bx in range(blocks[0]):
        for by in range(blocks[1]):
            entry = map_ref[bx, by, edge_block]
            here = (lane % cx // 8 == bx) & (row // 8 == by)
            mu_edge = jnp.where(here, table_ref[entry, 1], mu_edge)
            lm_edge = jnp.where(here, table_ref[entry, 0] + table_ref[entry, 1], lm_edge)

    def pack(packed, value, c, x):
        spot = c * cx + x
        moved = pltpu.roll(value, lax.rem(spot - edge + cz, cz), 1)
        return jnp.where(lane == spot, moved, packed)

    def fold(value):
        return value[:8] + value[8:]

    def to_row(accs):
        tall = jnp.concatenate([jnp.sum(a, 0, keepdims=True) for a in accs] + [jnp.zeros((2, cz), f32)], 0)
        total = jnp.sum(tall, 1, keepdims=True)
        spots = lax.broadcasted_iota(jnp.int32, (8, cz), 0) == lax.broadcasted_iota(jnp.int32, (8, cz), 1)
        return jnp.sum(jnp.where(spots, total, 0.0), 0, keepdims=True)

    rows = pl.ds(TOP, cy)
    zero_acc = tuple(jnp.zeros((8, cz), f32) for _ in range(6))

    def convert(x, carry):
        packed, accs = carry
        m = mask_s[x]
        grown = []
        for c in range(6):
            v = warm_ref[c, x].astype(f32)
            f0[c, x + 1, rows, :] = v
            grown.append(accs[c] + fold(m * v))
            packed = pack(packed, v, c, x)
        return packed, tuple(grown)

    packed, accs = lax.fori_loop(0, cx, convert, (jnp.zeros((cy, cz), f32), zero_acc))
    zsend0[...] = packed
    msg0[...] = to_row(accs)

    has = {"xm": gx > 0, "xp": gx < n_gx - 1, "ym": gy > 0, "yp": gy < n_gy - 1}

    def both(a, b):
        return jnp.logical_and(has[a], has[b])

    sources = [
        (has["xm"], -1, 0, False), (has["xp"], 1, 0, False),
        (has["ym"], 0, -1, False), (has["yp"], 0, 1, False),
        (both("xm", "ym"), -1, -1, False), (both("xm", "yp"), -1, 1, False),
        (both("xp", "ym"), 1, -1, False), (both("xp", "yp"), 1, 1, False),
        (None, 0, 0, True),
        (has["xm"], -1, 0, True), (has["xp"], 1, 0, True),
        (has["ym"], 0, -1, True), (has["yp"], 0, 1, True),
    ]

    def halo_part(field, dx, dy, halo):
        if dx == 0:
            px = pl.ds(1, cx)
        elif halo:
            px = pl.ds(0 if dx < 0 else cx + 1, 1)
        else:
            px = pl.ds(1 if dx < 0 else cx, 1)
        if dy == 0:
            py = pl.ds(TOP, cy)
        elif halo:
            py = pl.ds(TOP - 1 if dy < 0 else TOP + cy, 1)
        else:
            py = pl.ds(TOP if dy < 0 else TOP + cy - 1, 1)
        return field.at[:, px, py, :]

    def exchange(phase, field, zsend, zbuf):
        result = []
        for k, (cond, dx, dy, flip) in enumerate(sources):
            opposite = next(
                j for j, s in enumerate(sources) if s[1] == -dx and s[2] == -dy and s[3] == flip
            )
            if flip:
                src = zsend
                dst = zbuf.at[opposite - 8]
                here = zbuf.at[k - 8]
            else:
                src = halo_part(field, dx, dy, False)
                dst = halo_part(field, -dx, -dy, True)
                here = halo_part(field, dx, dy, True)
            target = {"gx": gx + dx, "gy": gy + dy, "col": 1 - col if flip else col}
            out = pltpu.make_async_remote_copy(
                src_ref=src, dst_ref=dst, send_sem=halo_send.at[phase, k],
                recv_sem=halo_recv.at[phase, opposite], device_id=target, device_id_type=MESH_ID,
            )
            arrive = pltpu.make_async_remote_copy(
                src_ref=here, dst_ref=here, send_sem=halo_send.at[phase, k],
                recv_sem=halo_recv.at[phase, k], device_id=target, device_id_type=MESH_ID,
            )
            result.append((cond, out, arrive))
        return result

    def guarded(cond, action):
        if cond is None:
            action()
        else:
            pl.when(cond)(action)

    def zero_absent(field, zbuf):
        for k, (cond, dx, dy, flip) in enumerate(sources):
            if cond is None:
                continue

            def clear(k=k, dx=dx, dy=dy, flip=flip):
                if flip:
                    zbuf[k - 8] = jnp.zeros(zbuf.shape[1:], f32)
                else:
                    part = halo_part(field, dx, dy, True)
                    part[...] = jnp.zeros(part.shape, f32)

            pl.when(jnp.logical_not(cond))(clear)

    def sum_copies(phase, msg, slots):
        result = []
        for p in range(1, group):
            other = peer(p)
            out = pltpu.make_async_remote_copy(
                src_ref=msg, dst_ref=slots.at[me], send_sem=sum_send.at[phase, p],
                recv_sem=sum_recv.at[phase, me], device_id=coords(other), device_id_type=MESH_ID,
            )
            arrive = pltpu.make_async_remote_copy(
                src_ref=msg, dst_ref=slots.at[other], send_sem=sum_send.at[phase, p],
                recv_sem=sum_recv.at[phase, other], device_id=coords(other), device_id_type=MESH_ID,
            )
            result.append((None, out, arrive))
        slots[me] = msg[...]
        return result

    zero_absent(f0, zbuf0)
    zero_absent(f1, zbuf1)

    pl.semaphore_wait(barrier, group - 1)

    pending = []

    def start(copies):
        for cond, out, _ in copies:
            guarded(cond, out.start)
        pending.extend(copies)

    def land(copies):
        for cond, _, arrive in copies:
            guarded(cond, arrive.wait_recv)

    halo0 = exchange(0, f0, zsend0, zbuf0)
    total0 = sum_copies(0, msg0, sums0)
    start(halo0)
    start(total0)

    load_density.wait()

    def prepare(x, carry):
        mu = mu_s[x // 8]
        lm = lm_s[x // 8]
        m = mask_s[x]
        inertia = omega * density_s[x].astype(f32)
        base = 6.0 * mu + 2.0 * lm - inertia
        for c in range(3):
            real = base + m * imp_ref[0, c]
            imag = m * imp_ref[1, c] - DAMPING * inertia
            scale = RELAXATION / (real * real + imag * imag)
            dinv[c, x] = real * scale
            dinv[3 + c, x] = imag * scale
        return carry

    lax.fori_loop(0, cx, prepare, 0)

    def shift_up(v):
        return jnp.where(lane == cz - 1, 0.0, pltpu.roll(v, cz - 1, 1))

    def shift_down(v):
        return jnp.where(lane == 0, 0.0, pltpu.roll(v, 1, 1))

    def z_terms(zbuf):
        sign = jnp.where(col == 0, 0.25, -0.25)
        h = zbuf[0]
        xs = lane % cx
        ahead = jnp.where(xs == cx - 1, pltpu.roll(zbuf[2], cx - 1, 1), pltpu.roll(h, cz - 1, 1))
        behind = jnp.where(xs == 0, pltpu.roll(zbuf[1], cz - cx + 1, 1), pltpu.roll(h, 1, 1))
        dxh = (ahead - behind) * sign
        above = jnp.where(row == cy - 1, pltpu.roll(zbuf[4], cy - 1, 0), pltpu.roll(h, cy - 1, 0))
        below = jnp.where(row == 0, pltpu.roll(zbuf[3], 1, 0), pltpu.roll(h, 1, 0))
        dyh = (above - below) * sign
        comp = lane // cx % 3
        extra = jnp.where(
            comp == 0,
            pltpu.roll(dxh, cz - 2 * cx, 1),
            jnp.where(
                comp == 1,
                pltpu.roll(dyh, cz - cx, 1),
                h + pltpu.roll(dxh, 2 * cx, 1) + pltpu.roll(dyh, cx, 1),
            ),
        )
        return mu_edge * h + lm_edge * extra

    def mean_terms(slots):
        total = jnp.sum(slots[...], 0) / jnp.float32(group * cells)
        means = [jnp.sum(jnp.where(lane1 == c, total, 0.0), 1, keepdims=True) for c in range(6)]
        result = []
        for c in range(3):
            result.append(imp_ref[0, c] * means[c] - imp_ref[1, c] * means[3 + c])
        for c in range(3):
            result.append(imp_ref[0, c] * means[3 + c] + imp_ref[1, c] * means[c])
        return [jnp.broadcast_to(r, (1, cz)) for r in result]

    def slope(field, part, px):
        uz = field[part + 2, px, rows, :]
        return (
            field[part + 1, px, pl.ds(TOP + 1, cy), :]
            - field[part + 1, px, pl.ds(TOP - 1, cy), :]
            + shift_up(uz)
            - shift_down(uz)
        )

    def update(field, x, slopes_before, slopes_after, zk, zm):
        px = x + 1
        mu = mu_s[x // 8]
        lm = lm_s[x // 8]
        quarter = 0.25 * lm
        m = mask_s[x]
        sums = []
        for part in (0, 3):
            xp = [field[part + c, px + 1, rows, :] for c in range(3)]
            xm = [field[part + c, px - 1, rows, :] for c in range(3)]
            yp = [field[part + c, px, pl.ds(TOP + 1, cy), :] for c in range(3)]
            ym = [field[part + c, px, pl.ds(TOP - 1, cy), :] for c in range(3)]
            mid = [field[part + c, px, rows, :] for c in range(3)]
            sx = [a + b for a, b in zip(xp, xm)]
            sy = [a + b for a, b in zip(yp, ym)]
            sz = [shift_up(v) + shift_down(v) for v in mid]
            own = [sx[0], sy[1], sz[2]]
            mixed_x = slopes_after[part // 3] - slopes_before[part // 3]
            dyz = yp[2] - ym[2]
            mixed_y = (
                (field[part, px + 1, pl.ds(TOP + 1, cy), :] - field[part, px - 1, pl.ds(TOP + 1, cy), :])
                - (field[part, px + 1, pl.ds(TOP - 1, cy), :] - field[part, px - 1, pl.ds(TOP - 1, cy), :])
                + shift_up(dyz)
                - shift_down(dyz)
            )
            across = (xp[0] - xm[0]) + (yp[1] - ym[1])
            mixed_z = shift_up(across) - shift_down(across)
            mixed = [mixed_x, mixed_y, mixed_z]
            for c in range(3):
                s = source_s[part + c, x].astype(f32)
                spot = (part + c) * cx + x
                beyond = pltpu.roll(zk, lax.rem(edge - spot + cz, cz), 1)
                s = s + jnp.where(lane == edge, beyond, 0.0)
                s = s + mu * (sx[c] + sy[c] + sz[c]) + lm * own[c] + quarter * mixed[c]
                sums.append(s + m * zm[part + c])
        result = [None] * 6
        for c in range(3):
            dr = dinv[c, x]
            di = dinv[3 + c, x]
            re, im = sums[c], sums[3 + c]
            result[c] = (1.0 - RELAXATION) * field[c, px, rows, :] + (re * dr + im * di)
            result[3 + c] = (1.0 - RELAXATION) * field[3 + c, px, rows, :] + (im * dr - re * di)
        return result, m

    def both_slopes(field, px):
        return (slope(field, 0, px), slope(field, 3, px))

    land(halo0)
    land(total0)
    load_source.wait()
    zk0 = z_terms(zbuf0)
    zm0 = mean_terms(sums0)

    def sweep_one(x, carry):
        before, centre, packed, accs = carry
        after = both_slopes(f0, x + 2)
        new, m = update(f0, x, before, after, zk0, zm0)
        grown = []
        for c in range(6):
            f1[c, x + 1, rows, :] = new[c]
            grown.append(accs[c] + fold(m * new[c]))
            packed = pack(packed, new[c], c, x)
        return centre, after, packed, tuple(grown)

    _, _, packed, accs = lax.fori_loop(
        0, cx, sweep_one,
        (both_slopes(f0, 0), both_slopes(f0, 1), jnp.zeros((cy, cz), f32), zero_acc),
    )
    zsend1[...] = packed
    halo1 = exchange(1, f1, zsend1, zbuf1)
    start(halo1)
    msg1[...] = to_row(accs)
    total1 = sum_copies(1, msg1, sums1)
    start(total1)

    load_forward.wait()
    land(halo1)
    land(total1)
    zk1 = z_terms(zbuf1)
    zm1 = mean_terms(sums1)

    def sweep_two(x, carry):
        before, centre, corr = carry
        after = both_slopes(f1, x + 2)
        new, _ = update(f1, x, before, after, zk1, zm1)
        for c in range(6):
            out_s[c, x] = new[c]
        for c in range(3):
            fr = forward_s[c, x].astype(f32)
            fi = forward_s[3 + c, x].astype(f32)
            corr = corr + (new[c] * (fr - DAMPING * fi) - new[3 + c] * (fi + DAMPING * fr))
        return centre, after, corr

    store = pltpu.make_async_copy(out_s, out_hbm, local_sem.at[3])
    carry = (both_slopes(f1, 0), both_slopes(f1, 1))
    bands = []
    for a in range(cx // 4):
        before, centre, corr = lax.fori_loop(
            4 * a, 4 * a + 4, sweep_two, carry + (jnp.zeros((cy, cz), f32),)
        )
        carry = (before, centre)
        bands.append(corr)
    store.start()
    tall = jnp.concatenate(bands, 0)
    n_rows = tall.shape[0]
    total = jnp.sum(tall, 1, keepdims=True) * (-omega / 64.0)
    spots = lax.broadcasted_iota(jnp.int32, (n_rows, cz), 1) == (
        lax.broadcasted_iota(jnp.int32, (n_rows, cz), 0) // 4 + gy * (n_rows // 4)
    )
    msg2[...] = jnp.sum(jnp.where(spots, total, 0.0), 0, keepdims=True)
    total2 = sum_copies(2, msg2, sums2)
    start(total2)
    land(total2)

    per_x, per_y = cx // 4, cy // 4
    shape = (n_gx * per_x, cz)
    lanes = lax.broadcasted_iota(jnp.int32, shape, 1)
    rows_out = lax.broadcasted_iota(jnp.int32, shape, 0)
    wide = jnp.zeros(shape, f32)
    for g in range(n_gx):
        strip = sums2[g * n_gy * n_col]
        for k in range(1, n_gy * n_col):
            strip = strip + sums2[g * n_gy * n_col + k]
        wide = jnp.where(rows_out // per_x == g, strip, wide)
    wide = jnp.where(lanes // per_y % per_x == rows_out % per_x, wide, 0.0)
    pick_shape = (cz, n_gy * per_y)
    source_lane = lax.broadcasted_iota(jnp.int32, pick_shape, 0)
    target_lane = lax.broadcasted_iota(jnp.int32, pick_shape, 1)
    pick = jnp.where(
        source_lane // (per_x * per_y) * per_y + source_lane % per_y == target_lane, 1.0, 0.0
    )
    coarse_ref[...] = lax.dot_general(
        wide, pick, (((1,), (0,)), ((), ())),
        preferred_element_type=f32, precision=lax.Precision.HIGHEST,
    )
    store.wait()
    for cond, out, _ in pending:
        guarded(cond, out.wait_send)


def shards(n_gx, n_gy, n_col, source, warm, forward, density, material_map, material_table,
           iface_cells, impedance, omega2):
    f32 = jnp.float32
    cx, cy, cz = density.shape
    group = n_gx * n_gy * n_col
    vmem = pl.BlockSpec(memory_space=pltpu.VMEM)
    smem = pl.BlockSpec(memory_space=pltpu.SMEM)
    hbm = pl.BlockSpec(memory_space=pl.ANY)
    field = pltpu.VMEM((6, cx + 2, TOP + cy + 8, cz), f32)
    tile = (cx, cy, cz)
    return pl.pallas_call(
        functools.partial(kernel, n_gx, n_gy, n_col),
        out_shape=(
            jax.ShapeDtypeStruct((6,) + tile, f32),
            jax.ShapeDtypeStruct((n_gx * (cx // 4), n_gy * (cy // 4)), f32),
        ),
        in_specs=[vmem, hbm, hbm, hbm, vmem, smem, smem, smem, smem],
        out_specs=(hbm, vmem),
        scratch_shapes=[
            field, field,
            pltpu.VMEM((5, cy, cz), f32), pltpu.VMEM((5, cy, cz), f32),
            pltpu.VMEM((cy, cz), f32), pltpu.VMEM((cy, cz), f32),
            pltpu.VMEM((group, 1, cz), f32), pltpu.VMEM((group, 1, cz), f32),
            pltpu.VMEM((group, 1, cz), f32),
            pltpu.VMEM((1, cz), f32), pltpu.VMEM((1, cz), f32), pltpu.VMEM((1, cz), f32),
            pltpu.VMEM(tile, f32),
            pltpu.VMEM((cx // 8, cy, cz), f32), pltpu.VMEM((cx // 8, cy, cz), f32),
            pltpu.VMEM((6,) + tile, f32),
            pltpu.VMEM((6,) + tile, jnp.bfloat16),
            pltpu.VMEM(tile, jnp.bfloat16),
            pltpu.VMEM((6,) + tile, jnp.bfloat16),
            pltpu.VMEM((6,) + tile, f32),
            pltpu.SemaphoreType.DMA((4,)),
            pltpu.SemaphoreType.DMA((2, 13)),
            pltpu.SemaphoreType.DMA((2, 13)),
            pltpu.SemaphoreType.DMA((3, group)),
            pltpu.SemaphoreType.DMA((3, group)),
        ],
        compiler_params=pltpu.CompilerParams(
            collective_id=0, has_side_effects=True, vmem_limit_bytes=32 * 1024 * 1024
        ),
        name="adjoint_sweeps",
    )(warm, source, density, forward, iface_cells, material_map, material_table, impedance, omega2)


def solution(mesh):
    in_specs = (
        P("freq", "gx", "gy", "col"),
        P("freq", "gx", "gy", "col"),
        P("freq", "gx", "gy", "col"),
        P("gx", "gy", "col"),
        P("gx", "gy", "col"),
        P(),
        P(("gx", "gy", "col"), None),
        P(),
        P("freq"),
    )
    out_specs = (P("freq", "gx", "gy", "col"), P("freq", None))
    body = functools.partial(shards, mesh.shape["gx"], mesh.shape["gy"], mesh.shape["col"])
    return jax.shard_map(body, mesh=mesh, in_specs=in_specs, out_specs=out_specs, check_vma=False)
```

```python
import functools
import jax
import jax.numpy as jnp
from jax import lax
from jax.experimental import pallas as pl
from jax.experimental.pallas import tpu as pltpu
from jax.sharding import PartitionSpec as P

DAMPING = 0.5
RELAXATION = 0.6
MESH_ID = pl.DeviceIdType.MESH
TOP = 8


def kernel(
    n_gx, n_gy, n_col,
    warm_hbm, source_hbm, density_hbm, forward_hbm, cells_ref,
    map_ref, table_ref, imp_ref, omega_ref,
    out_ref, coarse_ref,
    f0, f1, zbuf0, zbuf1, zsend0, zsend1, ybuf0, ybuf1, ysend0, ysend1,
    sums0, sums1, sums2, msg0, msg1, msg2,
    mask_s, mu_s, lm_s, dinv, warm_s, source_s, density_s, forward_s, part_s, ky_s,
    local_sem, halo_send, halo_recv, sum_send, sum_recv,
):
    f32 = jnp.float32
    cx, cy, cz = warm_hbm.shape[1:]
    cells = cells_ref.shape[1]
    group = n_gx * n_gy * n_col
    gx = lax.axis_index("gx")
    gy = lax.axis_index("gy")
    col = lax.axis_index("col")
    me = (gx * n_gy + gy) * n_col + col

    def coords(index):
        return {"gx": index // (n_gy * n_col), "gy": index // n_col % n_gy, "col": index % n_col}

    def peer(p):
        return lax.rem(me + p, group)

    barrier = pltpu.get_barrier_semaphore()
    for p in range(1, group):
        pl.semaphore_signal(barrier, inc=1, device_id=coords(peer(p)), device_id_type=MESH_ID)

    load_density = pltpu.make_async_copy(density_hbm, density_s, local_sem.at[0])
    load_source = pltpu.make_async_copy(source_hbm, source_s, local_sem.at[1])
    load_forward = pltpu.make_async_copy(forward_hbm, forward_s, local_sem.at[2])
    load_warm = pltpu.make_async_copy(warm_hbm, warm_s, local_sem.at[3])
    load_warm.start()
    load_density.start()
    load_source.start()
    load_forward.start()

    lane = lax.broadcasted_iota(jnp.int32, (cy, cz), 1)
    row = lax.broadcasted_iota(jnp.int32, (cy, cz), 0)
    lane1 = lax.broadcasted_iota(jnp.int32, (1, cz), 1)
    edge = jnp.where(col == 0, cz - 1, 0)
    omega = omega_ref[0]

    idx = cells_ref[...]
    hot_row = jnp.where(
        lax.broadcasted_iota(jnp.int32, (cx * cy, cells), 0) == idx // cz, 1.0, 0.0
    ).astype(jnp.bfloat16)
    hot_lane = jnp.where(
        lax.broadcasted_iota(jnp.int32, (cz, cells), 0) == idx % cz, 1.0, 0.0
    ).astype(jnp.bfloat16)
    mask = lax.dot_general(
        hot_row, hot_lane, (((1,), (1,)), ((), ())), preferred_element_type=f32
    )
    mask_s[...] = mask.reshape(cx, cy, cz)

    blocks = map_ref.shape
    for bx in range(blocks[0]):
        mus = []
        lms = []
        for by in range(blocks[1]):
            mu = jnp.zeros((8, cz), f32)
            lm = jnp.zeros((8, cz), f32)
            for bz in range(blocks[2]):
                entry = map_ref[bx, by, bz]
                here = lane[:8] // 32 == bz
                lm = jnp.where(here, table_ref[0, entry], lm)
                mu = jnp.where(here, table_ref[1, entry], mu)
            mus.append(mu)
            lms.append(lm + mu)
        mu_s[bx] = jnp.concatenate(mus, 0)
        lm_s[bx] = jnp.concatenate(lms, 0)
    mu_edge = jnp.zeros((cy, cz), f32)
    lm_edge = jnp.zeros((cy, cz), f32)
    edge_block = jnp.where(col == 0, blocks[2] - 1, 0)
    for bx in range(blocks[0]):
        for by in range(blocks[1]):
            entry = map_ref[bx, by, edge_block]
            here = (lane % cx // 8 == bx) & (row // 8 == by)
            mu_edge = jnp.where(here, table_ref[1, entry], mu_edge)
            lm_edge = jnp.where(here, table_ref[0, entry] + table_ref[1, entry], lm_edge)

    def pack(packed, value, c, x):
        spot = c * cx + x
        moved = pltpu.roll(value, lax.rem(spot - edge + cz, cz), 1)
        return jnp.where(lane == spot, moved, packed)

    def fold(value):
        return value[:8] + value[8:]

    def to_row(accs):
        tall = jnp.concatenate([jnp.sum(a, 0, keepdims=True) for a in accs] + [jnp.zeros((2, cz), f32)], 0)
        total = jnp.sum(tall, 1, keepdims=True)
        spots = lax.broadcasted_iota(jnp.int32, (8, cz), 0) == lax.broadcasted_iota(jnp.int32, (8, cz), 1)
        return jnp.sum(jnp.where(spots, total, 0.0), 0, keepdims=True)

    rows = pl.ds(TOP, cy)
    zero_acc = tuple(jnp.zeros((8, cz), f32) for _ in range(6))

    def convert(x, carry):
        packed, accs = carry
        m = mask_s[x]
        grown = []
        for c in range(6):
            v = warm_s[c, x].astype(f32)
            f0[c, x + 1, rows, :] = v
            ysend0[0, c, pl.ds(x, 1), :] = v[:1]
            ysend0[1, c, pl.ds(x, 1), :] = v[cy - 1 :]
            grown.append(accs[c] + fold(m * v))
            packed = pack(packed, v, c, x)
        return packed, tuple(grown)

    zero_rows = jnp.zeros((8, cz), f32)

    def clear_rows(x, carry):
        for field in (f0, f1):
            for c in range(6):
                field[c, x, pl.ds(0, 8), :] = zero_rows
                field[c, x, pl.ds(TOP + cy, 8), :] = zero_rows
        return carry

    lax.fori_loop(0, cx + 2, clear_rows, 0)
    load_warm.wait()
    packed, accs = lax.fori_loop(0, cx, convert, (jnp.zeros((cy, cz), f32), zero_acc))
    zsend0[...] = packed
    msg0[...] = to_row(accs)

    has = {"xm": gx > 0, "xp": gx < n_gx - 1, "ym": gy > 0, "yp": gy < n_gy - 1}

    def both(a, b):
        return jnp.logical_and(has[a], has[b])

    sources = [
        (has["xm"], -1, 0, False), (has["xp"], 1, 0, False),
        (has["ym"], 0, -1, False), (has["yp"], 0, 1, False),
        (both("xm", "ym"), -1, -1, False), (both("xm", "yp"), -1, 1, False),
        (both("xp", "ym"), 1, -1, False), (both("xp", "yp"), 1, 1, False),
        (None, 0, 0, True),
        (has["xm"], -1, 0, True), (has["xp"], 1, 0, True),
        (has["ym"], 0, -1, True), (has["yp"], 0, 1, True),
    ]

    def face(field, ysend, dx, dy):
        if dy == 0:
            return field.at[:, pl.ds(1 if dx < 0 else cx, 1), pl.ds(TOP, cy), :]
        spot = pl.ds(0, cx) if dx == 0 else pl.ds(0 if dx < 0 else cx - 1, 1)
        return ysend.at[0 if dy < 0 else 1, :, spot, :]

    def halo(field, ybuf, dx, dy):
        if dy == 0:
            return field.at[:, pl.ds(0 if dx < 0 else cx + 1, 1), pl.ds(TOP, cy), :]
        spot = pl.ds(TOP, cx) if dx == 0 else pl.ds(TOP - 1 if dx < 0 else TOP + cx, 1)
        return ybuf.at[0 if dy < 0 else 1, :, spot, :]

    def exchange(phase, field, ysend, ybuf, zsend, zbuf):
        result = []
        for k, (cond, dx, dy, flip) in enumerate(sources):
            opposite = next(
                j for j, s in enumerate(sources) if s[1] == -dx and s[2] == -dy and s[3] == flip
            )
            if flip:
                src = zsend
                dst = zbuf.at[opposite - 8]
                here = zbuf.at[k - 8]
            else:
                src = face(field, ysend, dx, dy)
                dst = halo(field, ybuf, -dx, -dy)
                here = halo(field, ybuf, dx, dy)
            target = {"gx": gx + dx, "gy": gy + dy, "col": 1 - col if flip else col}
            out = pltpu.make_async_remote_copy(
                src_ref=src, dst_ref=dst, send_sem=halo_send.at[phase, k],
                recv_sem=halo_recv.at[phase, opposite], device_id=target, device_id_type=MESH_ID,
            )
            arrive = pltpu.make_async_remote_copy(
                src_ref=here, dst_ref=here, send_sem=halo_send.at[phase, k],
                recv_sem=halo_recv.at[phase, k], device_id=target, device_id_type=MESH_ID,
            )
            result.append((cond, out, arrive))
        return result

    def guarded(cond, action):
        if cond is None:
            action()
        else:
            pl.when(cond)(action)

    def zero_absent(field, ybuf, zbuf):
        for k, (cond, dx, dy, flip) in enumerate(sources):
            if cond is None:
                continue

            def clear(k=k, dx=dx, dy=dy, flip=flip):
                if flip:
                    zbuf[k - 8] = jnp.zeros(zbuf.shape[1:], f32)
                else:
                    part = halo(field, ybuf, dx, dy)
                    part[...] = jnp.zeros(part.shape, f32)

            pl.when(jnp.logical_not(cond))(clear)

    def sum_copies(phase, msg, slots):
        result = []
        for p in range(1, group):
            other = peer(p)
            out = pltpu.make_async_remote_copy(
                src_ref=msg, dst_ref=slots.at[me], send_sem=sum_send.at[phase, p],
                recv_sem=sum_recv.at[phase, me], device_id=coords(other), device_id_type=MESH_ID,
            )
            arrive = pltpu.make_async_remote_copy(
                src_ref=msg, dst_ref=slots.at[other], send_sem=sum_send.at[phase, p],
                recv_sem=sum_recv.at[phase, other], device_id=coords(other), device_id_type=MESH_ID,
            )
            result.append((None, out, arrive))
        slots[me] = msg[...]
        return result

    zero_absent(f0, ybuf0, zbuf0)
    zero_absent(f1, ybuf1, zbuf1)

    pl.semaphore_wait(barrier, group - 1)

    pending = []

    def start(copies):
        for cond, out, _ in copies:
            guarded(cond, out.start)
        pending.extend(copies)

    def land(copies):
        for cond, _, arrive in copies:
            guarded(cond, arrive.wait_recv)

    halo0 = exchange(0, f0, ysend0, ybuf0, zsend0, zbuf0)
    total0 = sum_copies(0, msg0, sums0)
    start(halo0)
    start(total0)

    load_density.wait()

    def prepare(x, carry):
        mu = mu_s[x // 8]
        lm = lm_s[x // 8]
        m = mask_s[x]
        inertia = omega * density_s[x].astype(f32)
        base = 6.0 * mu + 2.0 * lm - inertia
        for c in range(3):
            real = base + m * imp_ref[0, c]
            imag = m * imp_ref[1, c] - DAMPING * inertia
            scale = RELAXATION / (real * real + imag * imag)
            dinv[c, x] = real * scale
            dinv[3 + c, x] = imag * scale
        return carry

    lax.fori_loop(0, cx, prepare, 0)

    def shift_up(v):
        return jnp.where(lane == cz - 1, 0.0, pltpu.roll(v, cz - 1, 1))

    def shift_down(v):
        return jnp.where(lane == 0, 0.0, pltpu.roll(v, 1, 1))

    def z_terms(zbuf):
        sign = jnp.where(col == 0, 0.25, -0.25)
        h = zbuf[0]
        xs = lane % cx
        ahead = jnp.where(xs == cx - 1, pltpu.roll(zbuf[2], cx - 1, 1), pltpu.roll(h, cz - 1, 1))
        behind = jnp.where(xs == 0, pltpu.roll(zbuf[1], cz - cx + 1, 1), pltpu.roll(h, 1, 1))
        dxh = (ahead - behind) * sign
        above = jnp.where(row == cy - 1, pltpu.roll(zbuf[4], cy - 1, 0), pltpu.roll(h, cy - 1, 0))
        below = jnp.where(row == 0, pltpu.roll(zbuf[3], 1, 0), pltpu.roll(h, 1, 0))
        dyh = (above - below) * sign
        comp = lane // cx % 3
        extra = jnp.where(
            comp == 0,
            pltpu.roll(dxh, cz - 2 * cx, 1),
            jnp.where(
                comp == 1,
                pltpu.roll(dyh, cz - cx, 1),
                h + pltpu.roll(dxh, 2 * cx, 1) + pltpu.roll(dyh, cx, 1),
            ),
        )
        return mu_edge * h + lm_edge * extra

    def mean_terms(slots):
        total = jnp.sum(slots[...], 0) / jnp.float32(group * cells)
        means = [jnp.sum(jnp.where(lane1 == c, total, 0.0), 1, keepdims=True) for c in range(6)]
        result = []
        for c in range(3):
            result.append(imp_ref[0, c] * means[c] - imp_ref[1, c] * means[3 + c])
        for c in range(3):
            result.append(imp_ref[0, c] * means[3 + c] + imp_ref[1, c] * means[c])
        return [jnp.broadcast_to(r, (1, cz)) for r in result]

    def slope(field, part, px):
        uz = field[part + 2, px, rows, :]
        return (
            field[part + 1, px, pl.ds(TOP + 1, cy), :]
            - field[part + 1, px, pl.ds(TOP - 1, cy), :]
            + shift_up(uz)
            - shift_down(uz)
        )

    def stencil(field, x, before, after):
        px = x + 1
        mu = mu_s[x // 8]
        lm = lm_s[x // 8]
        quarter = 0.25 * lm
        for part in (0, 3):
            xp = [field[part + c, px + 1, rows, :] for c in range(3)]
            xm = [field[part + c, px - 1, rows, :] for c in range(3)]
            yp = [field[part + c, px, pl.ds(TOP + 1, cy), :] for c in range(3)]
            ym = [field[part + c, px, pl.ds(TOP - 1, cy), :] for c in range(3)]
            mid = [field[part + c, px, rows, :] for c in range(3)]
            sx = [a + b for a, b in zip(xp, xm)]
            sy = [a + b for a, b in zip(yp, ym)]
            sz = [shift_up(v) + shift_down(v) for v in mid]
            own = [sx[0], sy[1], sz[2]]
            mixed_x = after[part // 3] - before[part // 3]
            dyz = yp[2] - ym[2]
            mixed_y = (
                (field[part, px + 1, pl.ds(TOP + 1, cy), :] - field[part, px - 1, pl.ds(TOP + 1, cy), :])
                - (field[part, px + 1, pl.ds(TOP - 1, cy), :] - field[part, px - 1, pl.ds(TOP - 1, cy), :])
                + shift_up(dyz)
                - shift_down(dyz)
            )
            across = (xp[0] - xm[0]) + (yp[1] - ym[1])
            mixed_z = shift_up(across) - shift_down(across)
            mixed = [mixed_x, mixed_y, mixed_z]
            for c in range(3):
                s = source_s[part + c, x].astype(f32)
                s = s + mu * (sx[c] + sy[c] + sz[c]) + lm * own[c] + quarter * mixed[c]
                part_s[part + c, x] = s

    def y_terms(ybuf):
        for side, edge_rows, sign in ((0, pl.ds(0, 8), -0.25), (1, pl.ds(cy - 8, 8), 0.25)):
            mu = jnp.concatenate([mu_s[bx, edge_rows, :] for bx in range(cx // 8)], 0)
            lm = jnp.concatenate([lm_s[bx, edge_rows, :] for bx in range(cx // 8)], 0)
            scaled = lm * sign
            for part in (0, 3):
                h = [ybuf[side, part + c, pl.ds(TOP, cx), :] for c in range(3)]
                dx = [
                    ybuf[side, part + c, pl.ds(TOP + 1, cx), :]
                    - ybuf[side, part + c, pl.ds(TOP - 1, cx), :]
                    for c in range(2)
                ]
                dz = [shift_up(h[c]) - shift_down(h[c]) for c in (1, 2)]
                ky_s[side, part] = mu * h[0] + scaled * dx[1]
                ky_s[side, part + 1] = (mu + lm) * h[1] + scaled * (dx[0] + dz[1])
                ky_s[side, part + 2] = mu * h[2] + scaled * dz[0]

    def finish(field, x, zk, zm):
        px = x + 1
        m = mask_s[x]
        sums = []
        for c in range(6):
            beyond = pltpu.roll(zk, lax.rem(edge - (c * cx + x) + cz, cz), 1)
            s = part_s[c, x] + jnp.where(lane == edge, beyond, 0.0)
            low = ky_s[0, c, pl.ds(x, 1), :]
            high = ky_s[1, c, pl.ds(x, 1), :]
            s = s + jnp.where(row == 0, low, jnp.where(row == cy - 1, high, 0.0))
            sums.append(s + m * zm[c])
        result = [None] * 6
        for c in range(3):
            dr = dinv[c, x]
            di = dinv[3 + c, x]
            re, im = sums[c], sums[3 + c]
            result[c] = (1.0 - RELAXATION) * field[c, px, rows, :] + (re * dr + im * di)
            result[3 + c] = (1.0 - RELAXATION) * field[3 + c, px, rows, :] + (im * dr - re * di)
        return result, m

    def both_slopes(field, px):
        return (slope(field, 0, px), slope(field, 3, px))

    def inner(field):
        def step(x, carry):
            before, centre = carry
            after = both_slopes(field, x + 2)
            stencil(field, x, before, after)
            return centre, after

        lax.fori_loop(1, cx - 1, step, (both_slopes(field, 1), both_slopes(field, 2)))

    def outer(field):
        def step(k, carry):
            x = k * (cx - 1)
            stencil(field, x, both_slopes(field, x), both_slopes(field, x + 2))
            return carry

        lax.fori_loop(0, 2, step, 0)

    load_source.wait()
    inner(f0)
    land(halo0)
    outer(f0)
    y_terms(ybuf0)
    zk0 = z_terms(zbuf0)
    land(total0)
    zm0 = mean_terms(sums0)

    def sweep_one(x, carry):
        packed, accs = carry
        new, m = finish(f0, x, zk0, zm0)
        grown = []
        for c in range(6):
            f1[c, x + 1, rows, :] = new[c]
            ysend1[0, c, pl.ds(x, 1), :] = new[c][:1]
            ysend1[1, c, pl.ds(x, 1), :] = new[c][cy - 1 :]
            grown.append(accs[c] + fold(m * new[c]))
            packed = pack(packed, new[c], c, x)
        return packed, tuple(grown)

    packed, accs = lax.fori_loop(0, cx, sweep_one, (jnp.zeros((cy, cz), f32), zero_acc))
    zsend1[...] = packed
    halo1 = exchange(1, f1, ysend1, ybuf1, zsend1, zbuf1)
    start(halo1)
    msg1[...] = to_row(accs)
    total1 = sum_copies(1, msg1, sums1)
    start(total1)

    inner(f1)
    load_forward.wait()
    land(halo1)
    outer(f1)
    y_terms(ybuf1)
    zk1 = z_terms(zbuf1)
    land(total1)
    zm1 = mean_terms(sums1)

    def sweep_two(x, corr):
        new, _ = finish(f1, x, zk1, zm1)
        for c in range(6):
            out_ref[c, x] = new[c]
        for c in range(3):
            fr = forward_s[c, x].astype(f32)
            fi = forward_s[3 + c, x].astype(f32)
            corr = corr + (new[c] * (fr - DAMPING * fi) - new[3 + c] * (fi + DAMPING * fr))
        return corr

    bands = [
        lax.fori_loop(4 * a, 4 * a + 4, sweep_two, jnp.zeros((cy, cz), f32)) for a in range(cx // 4)
    ]
    tall = jnp.concatenate(bands, 0)
    n_rows = tall.shape[0]
    total = jnp.sum(tall, 1, keepdims=True) * (-omega / 64.0)
    spots = lax.broadcasted_iota(jnp.int32, (n_rows, cz), 1) == (
        lax.broadcasted_iota(jnp.int32, (n_rows, cz), 0) // 4 + gy * (n_rows // 4)
    )
    msg2[...] = jnp.sum(jnp.where(spots, total, 0.0), 0, keepdims=True)
    total2 = sum_copies(2, msg2, sums2)
    start(total2)
    land(total2)

    per_x, per_y = cx // 4, cy // 4
    shape = (n_gx * per_x, cz)
    lanes = lax.broadcasted_iota(jnp.int32, shape, 1)
    rows_out = lax.broadcasted_iota(jnp.int32, shape, 0)
    wide = jnp.zeros(shape, f32)
    for g in range(n_gx):
        strip = sums2[g * n_gy * n_col]
        for k in range(1, n_gy * n_col):
            strip = strip + sums2[g * n_gy * n_col + k]
        wide = jnp.where(rows_out // per_x == g, strip, wide)
    wide = jnp.where(lanes // per_y % per_x == rows_out % per_x, wide, 0.0)
    pick_shape = (n_gy * per_y, cz)
    target = lax.broadcasted_iota(jnp.int32, pick_shape, 0)
    origin = lax.broadcasted_iota(jnp.int32, pick_shape, 1)
    pick = jnp.where(origin // (per_x * per_y) * per_y + origin % per_y == target, 1.0, 0.0)
    coarse_ref[...] = lax.dot_general(
        pick, wide, (((1,), (1,)), ((), ())),
        preferred_element_type=f32, precision=lax.Precision.HIGHEST,
    )
    for cond, out, _ in pending:
        guarded(cond, out.wait_send)


def shards(n_gx, n_gy, n_col, source, warm, forward, density, material_map, material_table,
           iface_cells, impedance, omega2):
    f32 = jnp.float32
    cx, cy, cz = density.shape
    group = n_gx * n_gy * n_col
    vmem = pl.BlockSpec(memory_space=pltpu.VMEM)
    smem = pl.BlockSpec(memory_space=pltpu.SMEM)
    hbm = pl.BlockSpec(memory_space=pltpu.HBM)
    field = pltpu.VMEM((6, cx + 2, TOP + cy + 8, cz), f32)
    tile = (cx, cy, cz)
    y_halo = pltpu.VMEM((2, 6, TOP + cx + 8, cz), f32)
    y_face = pltpu.VMEM((2, 6, cx, cz), f32)
    table = material_table.T
    warm, source, density, forward, iface_cells, material_map, table, impedance = (
        pltpu.with_memory_space_constraint(a, pltpu.HBM)
        for a in (warm, source, density, forward, iface_cells, material_map, table, impedance)
    )
    adjoint, coarse = pl.pallas_call(
        functools.partial(kernel, n_gx, n_gy, n_col),
        out_shape=(
            jax.ShapeDtypeStruct((6,) + tile, f32),
            jax.ShapeDtypeStruct((n_gy * (cy // 4), n_gx * (cx // 4)), f32),
        ),
        in_specs=[hbm, hbm, hbm, hbm, vmem, smem, smem, smem, smem],
        out_specs=(vmem, vmem),
        scratch_shapes=[
            field, field,
            pltpu.VMEM((5, cy, cz), f32), pltpu.VMEM((5, cy, cz), f32),
            pltpu.VMEM((cy, cz), f32), pltpu.VMEM((cy, cz), f32),
            y_halo, y_halo, y_face, y_face,
            pltpu.VMEM((group, 1, cz), f32), pltpu.VMEM((group, 1, cz), f32),
            pltpu.VMEM((group, 1, cz), f32),
            pltpu.VMEM((1, cz), f32), pltpu.VMEM((1, cz), f32), pltpu.VMEM((1, cz), f32),
            pltpu.VMEM(tile, f32),
            pltpu.VMEM((cx // 8, cy, cz), f32), pltpu.VMEM((cx // 8, cy, cz), f32),
            pltpu.VMEM((6,) + tile, f32),
            pltpu.VMEM((6,) + tile, jnp.bfloat16),
            pltpu.VMEM((6,) + tile, jnp.bfloat16),
            pltpu.VMEM(tile, jnp.bfloat16),
            pltpu.VMEM((6,) + tile, jnp.bfloat16),
            pltpu.VMEM((6,) + tile, f32),
            y_face,
            pltpu.SemaphoreType.DMA((4,)),
            pltpu.SemaphoreType.DMA((2, 13)),
            pltpu.SemaphoreType.DMA((2, 13)),
            pltpu.SemaphoreType.DMA((3, group)),
            pltpu.SemaphoreType.DMA((3, group)),
        ],
        compiler_params=pltpu.CompilerParams(
            collective_id=0, has_side_effects=True, vmem_limit_bytes=32 * 1024 * 1024
        ),
        name="adjoint_sweeps",
    )(warm, source, density, forward, iface_cells, material_map, table, impedance, omega2)
    return adjoint, coarse.T


def solution(mesh):
    in_specs = (
        P("freq", "gx", "gy", "col"),
        P("freq", "gx", "gy", "col"),
        P("freq", "gx", "gy", "col"),
        P("gx", "gy", "col"),
        P("gx", "gy", "col"),
        P(),
        P(("gx", "gy", "col"), None),
        P(),
        P("freq"),
    )
    out_specs = (P("freq", "gx", "gy", "col"), P("freq", None))
    body = functools.partial(shards, mesh.shape["gx"], mesh.shape["gy"], mesh.shape["col"])
    return jax.shard_map(body, mesh=mesh, in_specs=in_specs, out_specs=out_specs, check_vma=False)
```

```python
import functools
import jax
import jax.numpy as jnp
from jax import lax
from jax.experimental import pallas as pl
from jax.experimental.pallas import tpu as pltpu
from jax.sharding import PartitionSpec as P

DAMPING = 0.5
RELAXATION = 0.6
MESH_ID = pl.DeviceIdType.MESH
TOP = 8


def kernel(
    n_gx, n_gy, n_col,
    warm_hbm, source_hbm, density_hbm, forward_hbm, cells_ref,
    map_ref, table_ref, imp_ref, omega_ref,
    out_ref, coarse_ref,
    f0, f1, zbuf0, zbuf1, zsend0, zsend1, ybuf0, ybuf1, ysend0, ysend1,
    sums0, sums1, sums2, msg0, msg1, msg2,
    mask_s, mu_s, lm_s, dinv, warm_s, source_s, density_s, forward_s, part_s, ky_s,
    local_sem, halo_send, halo_recv, sum_send, sum_recv,
):
    f32 = jnp.float32
    cx, cy, cz = warm_hbm.shape[1:]
    cells = cells_ref.shape[1]
    group = n_gx * n_gy * n_col
    gx = lax.axis_index("gx")
    gy = lax.axis_index("gy")
    col = lax.axis_index("col")
    me = (gx * n_gy + gy) * n_col + col

    def turned(position, length):
        steps = [position + d for d in range(length)]
        return [steps[0]] + [jnp.where(t >= length, t - length, t) for t in steps[1:]]

    peers = []
    for other_gx in turned(gx, n_gx):
        for other_gy in turned(gy, n_gy):
            for other_col in turned(col, n_col):
                peers.append({"gx": other_gx, "gy": other_gy, "col": other_col})
    peers = peers[1:]

    barrier = pltpu.get_barrier_semaphore()
    for other in peers:
        pl.semaphore_signal(barrier, inc=1, device_id=other, device_id_type=MESH_ID)

    load_density = pltpu.make_async_copy(density_hbm, density_s, local_sem.at[0])
    load_source = pltpu.make_async_copy(source_hbm, source_s, local_sem.at[1])
    load_forward = pltpu.make_async_copy(forward_hbm, forward_s, local_sem.at[2])
    load_warm = pltpu.make_async_copy(warm_hbm, warm_s, local_sem.at[3])
    load_warm.start()
    load_density.start()
    load_source.start()
    load_forward.start()

    lane = lax.broadcasted_iota(jnp.int32, (cy, cz), 1)
    row = lax.broadcasted_iota(jnp.int32, (cy, cz), 0)
    lane1 = lax.broadcasted_iota(jnp.int32, (1, cz), 1)
    edge = jnp.where(col == 0, cz - 1, 0)
    omega = omega_ref[0]

    idx = cells_ref[...]
    hot_row = jnp.where(
        lax.broadcasted_iota(jnp.int32, (cx * cy, cells), 0) == lax.shift_right_logical(idx, cz.bit_length() - 1), 1.0, 0.0
    ).astype(jnp.bfloat16)
    hot_lane = jnp.where(
        lax.broadcasted_iota(jnp.int32, (cz, cells), 0) == (idx & (cz - 1)), 1.0, 0.0
    ).astype(jnp.bfloat16)
    mask = lax.dot_general(
        hot_row, hot_lane, (((1,), (1,)), ((), ())), preferred_element_type=f32
    )
    mask_s[...] = mask.reshape(cx, cy, cz)

    blocks = map_ref.shape
    for bx in range(blocks[0]):
        mus = []
        lms = []
        for by in range(blocks[1]):
            mu = jnp.zeros((8, cz), f32)
            lm = jnp.zeros((8, cz), f32)
            for bz in range(blocks[2]):
                entry = map_ref[bx, by, bz]
                here = (lane[:8] >= 32 * bz) & (lane[:8] < 32 * (bz + 1))
                lm = jnp.where(here, table_ref[0, entry], lm)
                mu = jnp.where(here, table_ref[1, entry], mu)
            mus.append(mu)
            lms.append(lm + mu)
        mu_s[bx] = jnp.concatenate(mus, 0)
        lm_s[bx] = jnp.concatenate(lms, 0)
    xs = lane & (cx - 1)
    mu_edge = jnp.zeros((cy, cz), f32)
    lm_edge = jnp.zeros((cy, cz), f32)
    edge_block = jnp.where(col == 0, blocks[2] - 1, 0)
    for bx in range(blocks[0]):
        for by in range(blocks[1]):
            entry = map_ref[bx, by, edge_block]
            here = ((xs >= 8 * bx) & (xs < 8 * (bx + 1))) & ((row >= 8 * by) & (row < 8 * (by + 1)))
            mu_edge = jnp.where(here, table_ref[1, entry], mu_edge)
            lm_edge = jnp.where(here, table_ref[0, entry] + table_ref[1, entry], lm_edge)

    def pack(packed, value, c, x):
        spot = c * cx + x
        moved = pltpu.roll(value, (spot - edge) & (cz - 1), 1)
        return jnp.where(lane == spot, moved, packed)

    def fold(value):
        return value[:8] + value[8:]

    def to_row(accs):
        tall = jnp.concatenate([jnp.sum(a, 0, keepdims=True) for a in accs] + [jnp.zeros((2, cz), f32)], 0)
        total = jnp.sum(tall, 1, keepdims=True)
        spots = lax.broadcasted_iota(jnp.int32, (8, cz), 0) == lax.broadcasted_iota(jnp.int32, (8, cz), 1)
        return jnp.sum(jnp.where(spots, total, 0.0), 0, keepdims=True)

    rows = pl.ds(TOP, cy)
    zero_acc = tuple(jnp.zeros((8, cz), f32) for _ in range(6))

    def convert(x, carry):
        packed, accs = carry
        clear_rows(x + 1)
        m = mask_s[x]
        grown = []
        for c in range(6):
            v = warm_s[c, x].astype(f32)
            f0[c, x + 1, rows, :] = v
            ysend0[0, c, pl.ds(x, 1), :] = v[:1]
            ysend0[1, c, pl.ds(x, 1), :] = v[cy - 1 :]
            grown.append(accs[c] + fold(m * v))
            packed = pack(packed, v, c, x)
        return packed, tuple(grown)

    zero_rows = jnp.zeros((8, cz), f32)

    def clear_rows(px):
        for field in (f0, f1):
            for c in range(6):
                field[c, px, pl.ds(0, 8), :] = zero_rows
                field[c, px, pl.ds(TOP + cy, 8), :] = zero_rows

    clear_rows(0)
    clear_rows(cx + 1)
    load_warm.wait()
    packed, accs = lax.fori_loop(0, cx, convert, (jnp.zeros((cy, cz), f32), zero_acc), unroll=2)
    zsend0[...] = packed
    msg0[...] = to_row(accs)

    has = {"xm": gx > 0, "xp": gx < n_gx - 1, "ym": gy > 0, "yp": gy < n_gy - 1}

    def both(a, b):
        return jnp.logical_and(has[a], has[b])

    sources = [
        (has["xm"], -1, 0, False), (has["xp"], 1, 0, False),
        (has["ym"], 0, -1, False), (has["yp"], 0, 1, False),
        (both("xm", "ym"), -1, -1, False), (both("xm", "yp"), -1, 1, False),
        (both("xp", "ym"), 1, -1, False), (both("xp", "yp"), 1, 1, False),
        (None, 0, 0, True),
        (has["xm"], -1, 0, True), (has["xp"], 1, 0, True),
        (has["ym"], 0, -1, True), (has["yp"], 0, 1, True),
    ]

    def face(field, ysend, dx, dy):
        if dy == 0:
            return field.at[:, pl.ds(1 if dx < 0 else cx, 1), pl.ds(TOP, cy), :]
        spot = pl.ds(0, cx) if dx == 0 else pl.ds(0 if dx < 0 else cx - 1, 1)
        return ysend.at[0 if dy < 0 else 1, :, spot, :]

    def halo(field, ybuf, dx, dy):
        if dy == 0:
            return field.at[:, pl.ds(0 if dx < 0 else cx + 1, 1), pl.ds(TOP, cy), :]
        spot = pl.ds(TOP, cx) if dx == 0 else pl.ds(TOP - 1 if dx < 0 else TOP + cx, 1)
        return ybuf.at[0 if dy < 0 else 1, :, spot, :]

    def exchange(phase, field, ysend, ybuf, zsend, zbuf):
        result = []
        for k, (cond, dx, dy, flip) in enumerate(sources):
            opposite = next(
                j for j, s in enumerate(sources) if s[1] == -dx and s[2] == -dy and s[3] == flip
            )
            if flip:
                src = zsend
                dst = zbuf.at[opposite - 8]
                here = zbuf.at[k - 8]
            else:
                src = face(field, ysend, dx, dy)
                dst = halo(field, ybuf, -dx, -dy)
                here = halo(field, ybuf, dx, dy)
            target = {"gx": gx + dx, "gy": gy + dy, "col": 1 - col if flip else col}
            out = pltpu.make_async_remote_copy(
                src_ref=src, dst_ref=dst, send_sem=halo_send.at[phase, k],
                recv_sem=halo_recv.at[phase, opposite], device_id=target, device_id_type=MESH_ID,
            )
            arrive = pltpu.make_async_remote_copy(
                src_ref=here, dst_ref=here, send_sem=halo_send.at[phase, k],
                recv_sem=halo_recv.at[phase, k], device_id=target, device_id_type=MESH_ID,
            )
            result.append((cond, out, arrive))
        return result

    def guarded(cond, action):
        if cond is None:
            action()
        else:
            pl.when(cond)(action)

    def zero_absent(field, ybuf, zbuf):
        for k, (cond, dx, dy, flip) in enumerate(sources):
            if cond is None:
                continue

            def clear(k=k, dx=dx, dy=dy, flip=flip):
                if flip:
                    zbuf[k - 8] = jnp.zeros(zbuf.shape[1:], f32)
                else:
                    part = halo(field, ybuf, dx, dy)
                    part[...] = jnp.zeros(part.shape, f32)

            pl.when(jnp.logical_not(cond))(clear)

    def sum_copies(phase, msg, slots):
        for other in peers:
            pltpu.make_async_remote_copy(
                src_ref=msg, dst_ref=slots.at[me], send_sem=sum_send.at[phase],
                recv_sem=sum_recv.at[phase], device_id=other, device_id_type=MESH_ID,
            ).start()
        slots[me] = msg[...]
        rest = slots.at[pl.ds(0, group - 1)]
        return pltpu.make_async_remote_copy(
            src_ref=rest, dst_ref=rest, send_sem=sum_send.at[phase],
            recv_sem=sum_recv.at[phase], device_id=peers[0], device_id_type=MESH_ID,
        )

    zero_absent(f0, ybuf0, zbuf0)
    zero_absent(f1, ybuf1, zbuf1)

    pl.semaphore_wait(barrier, group - 1)

    pending = []

    def start(copies):
        for cond, out, _ in copies:
            guarded(cond, out.start)
        pending.extend(copies)

    def land(copies):
        for cond, _, arrive in copies:
            guarded(cond, arrive.wait_recv)

    halo0 = exchange(0, f0, ysend0, ybuf0, zsend0, zbuf0)
    start(halo0)
    total0 = sum_copies(0, msg0, sums0)

    load_density.wait()

    def prepare(x, carry):
        mu = mu_s[lax.shift_right_logical(x, 3)]
        lm = lm_s[lax.shift_right_logical(x, 3)]
        m = mask_s[x]
        inertia = omega * density_s[x].astype(f32)
        base = 6.0 * mu + 2.0 * lm - inertia
        for c in range(3):
            real = base + m * imp_ref[0, c]
            imag = m * imp_ref[1, c] - DAMPING * inertia
            scale = RELAXATION / (real * real + imag * imag)
            dinv[c, x] = real * scale
            dinv[3 + c, x] = imag * scale
        return carry

    lax.fori_loop(0, cx, prepare, 0, unroll=2)

    def shift_up(v):
        return jnp.where(lane == cz - 1, 0.0, pltpu.roll(v, cz - 1, 1))

    def shift_down(v):
        return jnp.where(lane == 0, 0.0, pltpu.roll(v, 1, 1))

    def z_terms(zbuf):
        sign = jnp.where(col == 0, 0.25, -0.25)
        h = zbuf[0]
        ahead = jnp.where(xs == cx - 1, pltpu.roll(zbuf[2], cx - 1, 1), pltpu.roll(h, cz - 1, 1))
        behind = jnp.where(xs == 0, pltpu.roll(zbuf[1], cz - cx + 1, 1), pltpu.roll(h, 1, 1))
        dxh = (ahead - behind) * sign
        above = jnp.where(row == cy - 1, pltpu.roll(zbuf[4], cy - 1, 0), pltpu.roll(h, cy - 1, 0))
        below = jnp.where(row == 0, pltpu.roll(zbuf[3], 1, 0), pltpu.roll(h, 1, 0))
        dyh = (above - below) * sign

        def block(c):
            own = (lane >= c * cx) & (lane < (c + 1) * cx)
            return own | ((lane >= (c + 3) * cx) & (lane < (c + 4) * cx))

        extra = jnp.where(
            block(0),
            pltpu.roll(dxh, cz - 2 * cx, 1),
            jnp.where(
                block(1),
                pltpu.roll(dyh, cz - cx, 1),
                h + pltpu.roll(dxh, 2 * cx, 1) + pltpu.roll(dyh, cx, 1),
            ),
        )
        return mu_edge * h + lm_edge * extra

    def mean_terms(slots):
        total = jnp.sum(slots[...], 0) / jnp.float32(group * cells)
        means = [jnp.sum(jnp.where(lane1 == c, total, 0.0), 1, keepdims=True) for c in range(6)]
        result = []
        for c in range(3):
            result.append(imp_ref[0, c] * means[c] - imp_ref[1, c] * means[3 + c])
        for c in range(3):
            result.append(imp_ref[0, c] * means[3 + c] + imp_ref[1, c] * means[c])
        return [jnp.broadcast_to(r, (1, cz)) for r in result]

    def slope(field, part, px):
        uz = field[part + 2, px, rows, :]
        return (
            field[part + 1, px, pl.ds(TOP + 1, cy), :]
            - field[part + 1, px, pl.ds(TOP - 1, cy), :]
            + shift_up(uz)
            - shift_down(uz)
        )

    def stencil(field, x, before, after):
        px = x + 1
        mu = mu_s[lax.shift_right_logical(x, 3)]
        lm = lm_s[lax.shift_right_logical(x, 3)]
        quarter = 0.25 * lm
        for part in (0, 3):
            xp = [field[part + c, px + 1, rows, :] for c in range(3)]
            xm = [field[part + c, px - 1, rows, :] for c in range(3)]
            yp = [field[part + c, px, pl.ds(TOP + 1, cy), :] for c in range(3)]
            ym = [field[part + c, px, pl.ds(TOP - 1, cy), :] for c in range(3)]
            mid = [field[part + c, px, rows, :] for c in range(3)]
            sx = [a + b for a, b in zip(xp, xm)]
            sy = [a + b for a, b in zip(yp, ym)]
            sz = [shift_up(v) + shift_down(v) for v in mid]
            own = [sx[0], sy[1], sz[2]]
            mixed_x = after[part // 3] - before[part // 3]
            dyz = yp[2] - ym[2]
            mixed_y = (
                (field[part, px + 1, pl.ds(TOP + 1, cy), :] - field[part, px - 1, pl.ds(TOP + 1, cy), :])
                - (field[part, px + 1, pl.ds(TOP - 1, cy), :] - field[part, px - 1, pl.ds(TOP - 1, cy), :])
                + shift_up(dyz)
                - shift_down(dyz)
            )
            across = (xp[0] - xm[0]) + (yp[1] - ym[1])
            mixed_z = shift_up(across) - shift_down(across)
            mixed = [mixed_x, mixed_y, mixed_z]
            for c in range(3):
                s = source_s[part + c, x].astype(f32)
                s = s + mu * (sx[c] + sy[c] + sz[c]) + lm * own[c] + quarter * mixed[c]
                part_s[part + c, x] = s

    def y_terms(ybuf):
        for side, edge_rows, sign in ((0, pl.ds(0, 8), -0.25), (1, pl.ds(cy - 8, 8), 0.25)):
            mu = jnp.concatenate([mu_s[bx, edge_rows, :] for bx in range(cx // 8)], 0)
            lm = jnp.concatenate([lm_s[bx, edge_rows, :] for bx in range(cx // 8)], 0)
            scaled = lm * sign
            for part in (0, 3):
                h = [ybuf[side, part + c, pl.ds(TOP, cx), :] for c in range(3)]
                dx = [
                    ybuf[side, part + c, pl.ds(TOP + 1, cx), :]
                    - ybuf[side, part + c, pl.ds(TOP - 1, cx), :]
                    for c in range(2)
                ]
                dz = [shift_up(h[c]) - shift_down(h[c]) for c in (1, 2)]
                ky_s[side, part] = mu * h[0] + scaled * dx[1]
                ky_s[side, part + 1] = (mu + lm) * h[1] + scaled * (dx[0] + dz[1])
                ky_s[side, part + 2] = mu * h[2] + scaled * dz[0]

    def finish(field, x, zk, zm):
        px = x + 1
        m = mask_s[x]
        sums = []
        for c in range(6):
            beyond = pltpu.roll(zk, (edge - (c * cx + x)) & (cz - 1), 1)
            s = part_s[c, x] + jnp.where(lane == edge, beyond, 0.0)
            low = ky_s[0, c, pl.ds(x, 1), :]
            high = ky_s[1, c, pl.ds(x, 1), :]
            s = s + jnp.where(row == 0, low, jnp.where(row == cy - 1, high, 0.0))
            sums.append(s + m * zm[c])
        result = [None] * 6
        for c in range(3):
            dr = dinv[c, x]
            di = dinv[3 + c, x]
            re, im = sums[c], sums[3 + c]
            result[c] = (1.0 - RELAXATION) * field[c, px, rows, :] + (re * dr + im * di)
            result[3 + c] = (1.0 - RELAXATION) * field[3 + c, px, rows, :] + (im * dr - re * di)
        return result, m

    def both_slopes(field, px):
        return (slope(field, 0, px), slope(field, 3, px))

    def inner(field):
        def step(x, carry):
            before, centre = carry
            after = both_slopes(field, x + 2)
            stencil(field, x, before, after)
            return centre, after

        lax.fori_loop(1, cx - 1, step, (both_slopes(field, 1), both_slopes(field, 2)), unroll=2)

    def outer(field):
        def step(k, carry):
            x = k * (cx - 1)
            stencil(field, x, both_slopes(field, x), both_slopes(field, x + 2))
            return carry

        lax.fori_loop(0, 2, step, 0)

    load_source.wait()
    inner(f0)
    land(halo0)
    outer(f0)
    y_terms(ybuf0)
    zk0 = z_terms(zbuf0)
    total0.wait_recv()
    zm0 = mean_terms(sums0)

    def sweep_one(x, carry):
        packed, accs = carry
        new, m = finish(f0, x, zk0, zm0)
        grown = []
        for c in range(6):
            f1[c, x + 1, rows, :] = new[c]
            ysend1[0, c, pl.ds(x, 1), :] = new[c][:1]
            ysend1[1, c, pl.ds(x, 1), :] = new[c][cy - 1 :]
            grown.append(accs[c] + fold(m * new[c]))
            packed = pack(packed, new[c], c, x)
        return packed, tuple(grown)

    packed, accs = lax.fori_loop(
        0, cx, sweep_one, (jnp.zeros((cy, cz), f32), zero_acc), unroll=2
    )
    zsend1[...] = packed
    halo1 = exchange(1, f1, ysend1, ybuf1, zsend1, zbuf1)
    start(halo1)
    msg1[...] = to_row(accs)
    total1 = sum_copies(1, msg1, sums1)

    inner(f1)
    load_forward.wait()
    land(halo1)
    outer(f1)
    y_terms(ybuf1)
    zk1 = z_terms(zbuf1)
    total1.wait_recv()
    zm1 = mean_terms(sums1)

    def sweep_two(x, corr):
        new, _ = finish(f1, x, zk1, zm1)
        for c in range(6):
            out_ref[c, x] = new[c]
        for c in range(3):
            fr = forward_s[c, x].astype(f32)
            fi = forward_s[3 + c, x].astype(f32)
            corr = corr + (new[c] * (fr - DAMPING * fi) - new[3 + c] * (fi + DAMPING * fr))
        return corr

    bands = [
        lax.fori_loop(4 * a, 4 * a + 4, sweep_two, jnp.zeros((cy, cz), f32), unroll=2) for a in range(cx // 4)
    ]
    tall = jnp.concatenate(bands, 0)
    n_rows = tall.shape[0]
    band_sums = jnp.sum(tall, 1, keepdims=True) * (-omega / 64.0)
    spots = lax.broadcasted_iota(jnp.int32, (n_rows, cz), 1) == (
        lax.shift_right_logical(lax.broadcasted_iota(jnp.int32, (n_rows, cz), 0), 2) + gy * (n_rows // 4)
    )
    msg2[...] = jnp.sum(jnp.where(spots, band_sums, 0.0), 0, keepdims=True)
    total2 = sum_copies(2, msg2, sums2)
    per_x, per_y = cx // 4, cy // 4
    assert per_x == 4 and per_y == 4 and cx == 16 and cz == 128 and n_col == 2
    shape = (n_gx * per_x, cz)
    lanes = lax.broadcasted_iota(jnp.int32, shape, 1)
    rows_out = lax.broadcasted_iota(jnp.int32, shape, 0)
    keep = (lax.shift_right_logical(lanes, 2) & (per_x - 1)) == (rows_out & (per_x - 1))
    pick_shape = (n_gy * per_y, cz)
    target = lax.broadcasted_iota(jnp.int32, pick_shape, 0)
    origin = lax.broadcasted_iota(jnp.int32, pick_shape, 1)
    place = lax.shift_right_logical(origin, 4) * per_y + (origin & (per_y - 1))
    pick = jnp.where(place == target, 1.0, 0.0)
    total2.wait_recv()
    wide = jnp.zeros(shape, f32)
    for g in range(n_gx):
        strip = sums2[g * n_gy * n_col]
        for k in range(1, n_gy * n_col):
            strip = strip + sums2[g * n_gy * n_col + k]
        wide = jnp.where((rows_out >= g * per_x) & (rows_out < (g + 1) * per_x), strip, wide)
    wide = jnp.where(keep, wide, 0.0)
    coarse_ref[...] = lax.dot_general(
        pick, wide, (((1,), (1,)), ((), ())),
        preferred_element_type=f32, precision=lax.Precision.HIGHEST,
    )
    for cond, out, _ in pending:
        guarded(cond, out.wait_send)
    for total in (total0, total1, total2):
        total.wait_send()


def shards(n_gx, n_gy, n_col, source, warm, forward, density, material_map, material_table,
           iface_cells, impedance, omega2):
    f32 = jnp.float32
    cx, cy, cz = density.shape
    group = n_gx * n_gy * n_col
    vmem = pl.BlockSpec(memory_space=pltpu.VMEM)
    smem = pl.BlockSpec(memory_space=pltpu.SMEM)
    hbm = pl.BlockSpec(memory_space=pltpu.HBM)
    field = pltpu.VMEM((6, cx + 2, TOP + cy + 8, cz), f32)
    tile = (cx, cy, cz)
    y_halo = pltpu.VMEM((2, 6, TOP + cx + 8, cz), f32)
    y_face = pltpu.VMEM((2, 6, cx, cz), f32)
    table = material_table.T
    warm, source, density, forward, iface_cells, material_map, table, impedance = (
        pltpu.with_memory_space_constraint(a, pltpu.HBM)
        for a in (warm, source, density, forward, iface_cells, material_map, table, impedance)
    )
    adjoint, coarse = pl.pallas_call(
        functools.partial(kernel, n_gx, n_gy, n_col),
        out_shape=(
            jax.ShapeDtypeStruct((6,) + tile, f32),
            jax.ShapeDtypeStruct((n_gy * (cy // 4), n_gx * (cx // 4)), f32),
        ),
        in_specs=[hbm, hbm, hbm, hbm, vmem, smem, smem, smem, smem],
        out_specs=(vmem, vmem),
        scratch_shapes=[
            field, field,
            pltpu.VMEM((5, cy, cz), f32), pltpu.VMEM((5, cy, cz), f32),
            pltpu.VMEM((cy, cz), f32), pltpu.VMEM((cy, cz), f32),
            y_halo, y_halo, y_face, y_face,
            pltpu.VMEM((group, 1, cz), f32), pltpu.VMEM((group, 1, cz), f32),
            pltpu.VMEM((group, 1, cz), f32),
            pltpu.VMEM((1, cz), f32), pltpu.VMEM((1, cz), f32), pltpu.VMEM((1, cz), f32),
            pltpu.VMEM(tile, f32),
            pltpu.VMEM((cx // 8, cy, cz), f32), pltpu.VMEM((cx // 8, cy, cz), f32),
            pltpu.VMEM((6,) + tile, f32),
            pltpu.VMEM((6,) + tile, jnp.bfloat16),
            pltpu.VMEM((6,) + tile, jnp.bfloat16),
            pltpu.VMEM(tile, jnp.bfloat16),
            pltpu.VMEM((6,) + tile, jnp.bfloat16),
            pltpu.VMEM((6,) + tile, f32),
            y_face,
            pltpu.SemaphoreType.DMA((4,)),
            pltpu.SemaphoreType.DMA((2, 13)),
            pltpu.SemaphoreType.DMA((2, 13)),
            pltpu.SemaphoreType.DMA((3,)),
            pltpu.SemaphoreType.DMA((3,)),
        ],
        compiler_params=pltpu.CompilerParams(
            collective_id=0, has_side_effects=True, vmem_limit_bytes=32 * 1024 * 1024
        ),
        name="adjoint_sweeps",
    )(warm, source, density, forward, iface_cells, material_map, table, impedance, omega2)
    return adjoint, coarse.T


def solution(mesh):
    in_specs = (
        P("freq", "gx", "gy", "col"),
        P("freq", "gx", "gy", "col"),
        P("freq", "gx", "gy", "col"),
        P("gx", "gy", "col"),
        P("gx", "gy", "col"),
        P(),
        P(("gx", "gy", "col"), None),
        P(),
        P("freq"),
    )
    out_specs = (P("freq", "gx", "gy", "col"), P("freq", None))
    body = functools.partial(shards, mesh.shape["gx"], mesh.shape["gy"], mesh.shape["col"])
    return jax.shard_map(body, mesh=mesh, in_specs=in_specs, out_specs=out_specs, check_vma=False)
```

```python
import functools
import jax
import jax.numpy as jnp
from jax import lax
from jax.experimental import pallas as pl
from jax.experimental.pallas import tpu as pltpu
from jax.sharding import PartitionSpec as P

DAMPING = 0.5
RELAXATION = 0.6
MESH_ID = pl.DeviceIdType.MESH
TOP = 8


def kernel(
    n_gx, n_gy, n_col,
    warm_hbm, source_hbm, density_hbm, forward_hbm, cells_ref,
    map_ref, table_ref, imp_ref, omega_ref,
    out_ref, coarse_ref,
    f0, f1, zbuf0, zbuf1, zsend0, zsend1, ybuf0, ybuf1, ysend0, ysend1,
    sums0, sums1, sums2, msg0, msg1, msg2,
    mask_s, mu_s, lm_s, dinv, warm_s, source_s, density_s, forward_s, part_s, ky_s, slope_s,
    local_sem, halo_send, halo_recv, sum_send, sum_recv,
):
    f32 = jnp.float32
    cx, cy, cz = warm_hbm.shape[1:]
    cells = cells_ref.shape[1]
    group = n_gx * n_gy * n_col
    gx = lax.axis_index("gx")
    gy = lax.axis_index("gy")
    col = lax.axis_index("col")
    me = (gx * n_gy + gy) * n_col + col

    def turned(position, length):
        steps = [position + d for d in range(length)]
        return [steps[0]] + [jnp.where(t >= length, t - length, t) for t in steps[1:]]

    peers = []
    for other_gx in turned(gx, n_gx):
        for other_gy in turned(gy, n_gy):
            for other_col in turned(col, n_col):
                peers.append({"gx": other_gx, "gy": other_gy, "col": other_col})
    peers = peers[1:]

    barrier = pltpu.get_barrier_semaphore()
    for other in peers:
        pl.semaphore_signal(barrier, inc=1, device_id=other, device_id_type=MESH_ID)

    load_density = pltpu.make_async_copy(density_hbm, density_s, local_sem.at[0])
    load_source = pltpu.make_async_copy(source_hbm, source_s, local_sem.at[1])
    load_forward = pltpu.make_async_copy(forward_hbm, forward_s, local_sem.at[2])
    load_warm = pltpu.make_async_copy(warm_hbm, warm_s, local_sem.at[3])
    load_warm.start()
    load_density.start()
    load_source.start()
    load_forward.start()

    lane = lax.broadcasted_iota(jnp.int32, (cy, cz), 1)
    row = lax.broadcasted_iota(jnp.int32, (cy, cz), 0)
    lane1 = lax.broadcasted_iota(jnp.int32, (1, cz), 1)
    edge = jnp.where(col == 0, cz - 1, 0)
    omega = omega_ref[0]

    idx = cells_ref[...]
    hot_row = jnp.where(
        lax.broadcasted_iota(jnp.int32, (cx * cy, cells), 0) == lax.shift_right_logical(idx, cz.bit_length() - 1), 1.0, 0.0
    ).astype(jnp.bfloat16)
    hot_lane = jnp.where(
        lax.broadcasted_iota(jnp.int32, (cz, cells), 0) == (idx & (cz - 1)), 1.0, 0.0
    ).astype(jnp.bfloat16)
    mask = lax.dot_general(
        hot_row, hot_lane, (((1,), (1,)), ((), ())), preferred_element_type=f32
    )
    mask_s[...] = mask.reshape(cx, cy, cz)

    blocks = map_ref.shape
    for bx in range(blocks[0]):
        mus = []
        lms = []
        for by in range(blocks[1]):
            mu = jnp.zeros((8, cz), f32)
            lm = jnp.zeros((8, cz), f32)
            for bz in range(blocks[2]):
                entry = map_ref[bx, by, bz]
                here = (lane[:8] >= 32 * bz) & (lane[:8] < 32 * (bz + 1))
                lm = jnp.where(here, table_ref[0, entry], lm)
                mu = jnp.where(here, table_ref[1, entry], mu)
            mus.append(mu)
            lms.append(lm + mu)
        mu_s[bx] = jnp.concatenate(mus, 0)
        lm_s[bx] = jnp.concatenate(lms, 0)
    xs = lane & (cx - 1)
    mu_edge = jnp.zeros((cy, cz), f32)
    lm_edge = jnp.zeros((cy, cz), f32)
    edge_block = jnp.where(col == 0, blocks[2] - 1, 0)
    for bx in range(blocks[0]):
        for by in range(blocks[1]):
            entry = map_ref[bx, by, edge_block]
            here = ((xs >= 8 * bx) & (xs < 8 * (bx + 1))) & ((row >= 8 * by) & (row < 8 * (by + 1)))
            mu_edge = jnp.where(here, table_ref[1, entry], mu_edge)
            lm_edge = jnp.where(here, table_ref[0, entry] + table_ref[1, entry], lm_edge)

    def pack(packed, value, c, x):
        spot = c * cx + x
        moved = pltpu.roll(value, (spot - edge) & (cz - 1), 1)
        return jnp.where(lane == spot, moved, packed)

    def fold(value):
        return value[:8] + value[8:]

    def to_row(accs):
        tall = jnp.concatenate([jnp.sum(a, 0, keepdims=True) for a in accs] + [jnp.zeros((2, cz), f32)], 0)
        total = jnp.sum(tall, 1, keepdims=True)
        spots = lax.broadcasted_iota(jnp.int32, (8, cz), 0) == lax.broadcasted_iota(jnp.int32, (8, cz), 1)
        return jnp.sum(jnp.where(spots, total, 0.0), 0, keepdims=True)

    zero_acc = tuple(jnp.zeros((8, cz), f32) for _ in range(6))

    def convert(x, carry):
        packed, accs = carry
        m = mask_s[x]
        grown = []
        for c in range(6):
            v = warm_s[c, x].astype(f32)
            f0[c, x + 1] = v
            ysend0[0, c, pl.ds(x, 1), :] = v[:1]
            ysend0[1, c, pl.ds(x, 1), :] = v[cy - 1 :]
            grown.append(accs[c] + fold(m * v))
            packed = pack(packed, v, c, x)
        return packed, tuple(grown)


    load_warm.wait()
    packed, accs = lax.fori_loop(0, cx, convert, (jnp.zeros((cy, cz), f32), zero_acc), unroll=2)
    zsend0[...] = packed
    msg0[...] = to_row(accs)

    has = {"xm": gx > 0, "xp": gx < n_gx - 1, "ym": gy > 0, "yp": gy < n_gy - 1}

    def both(a, b):
        return jnp.logical_and(has[a], has[b])

    sources = [
        (has["xm"], -1, 0, False), (has["xp"], 1, 0, False),
        (has["ym"], 0, -1, False), (has["yp"], 0, 1, False),
        (both("xm", "ym"), -1, -1, False), (both("xm", "yp"), -1, 1, False),
        (both("xp", "ym"), 1, -1, False), (both("xp", "yp"), 1, 1, False),
        (None, 0, 0, True),
        (has["xm"], -1, 0, True), (has["xp"], 1, 0, True),
        (has["ym"], 0, -1, True), (has["yp"], 0, 1, True),
    ]

    def face(field, ysend, dx, dy):
        if dy == 0:
            return field.at[:, pl.ds(1 if dx < 0 else cx, 1)]
        spot = pl.ds(0, cx) if dx == 0 else pl.ds(0 if dx < 0 else cx - 1, 1)
        return ysend.at[0 if dy < 0 else 1, :, spot, :]

    def halo(field, ybuf, dx, dy):
        if dy == 0:
            return field.at[:, pl.ds(0 if dx < 0 else cx + 1, 1)]
        spot = pl.ds(TOP, cx) if dx == 0 else pl.ds(TOP - 1 if dx < 0 else TOP + cx, 1)
        return ybuf.at[0 if dy < 0 else 1, :, spot, :]

    def exchange(phase, field, ysend, ybuf, zsend, zbuf):
        result = []
        for k, (cond, dx, dy, flip) in enumerate(sources):
            opposite = next(
                j for j, s in enumerate(sources) if s[1] == -dx and s[2] == -dy and s[3] == flip
            )
            if flip:
                src = zsend
                dst = zbuf.at[opposite - 8]
                here = zbuf.at[k - 8]
            else:
                src = face(field, ysend, dx, dy)
                dst = halo(field, ybuf, -dx, -dy)
                here = halo(field, ybuf, dx, dy)
            target = {"gx": gx + dx, "gy": gy + dy, "col": 1 - col if flip else col}
            out = pltpu.make_async_remote_copy(
                src_ref=src, dst_ref=dst, send_sem=halo_send.at[phase, k],
                recv_sem=halo_recv.at[phase, opposite], device_id=target, device_id_type=MESH_ID,
            )
            arrive = pltpu.make_async_remote_copy(
                src_ref=here, dst_ref=here, send_sem=halo_send.at[phase, k],
                recv_sem=halo_recv.at[phase, k], device_id=target, device_id_type=MESH_ID,
            )
            result.append((cond, out, arrive))
        return result

    def guarded(cond, action):
        if cond is None:
            action()
        else:
            pl.when(cond)(action)

    def zero_absent(field, ybuf, zbuf):
        for k, (cond, dx, dy, flip) in enumerate(sources):
            if cond is None:
                continue

            def clear(k=k, dx=dx, dy=dy, flip=flip):
                if flip:
                    zbuf[k - 8] = jnp.zeros(zbuf.shape[1:], f32)
                else:
                    part = halo(field, ybuf, dx, dy)
                    part[...] = jnp.zeros(part.shape, f32)

            pl.when(jnp.logical_not(cond))(clear)

    def sum_copies(phase, msg, slots):
        for other in peers:
            pltpu.make_async_remote_copy(
                src_ref=msg, dst_ref=slots.at[me], send_sem=sum_send.at[phase],
                recv_sem=sum_recv.at[phase], device_id=other, device_id_type=MESH_ID,
            ).start()
        slots[me] = msg[...]
        rest = slots.at[pl.ds(0, group - 1)]
        return pltpu.make_async_remote_copy(
            src_ref=rest, dst_ref=rest, send_sem=sum_send.at[phase],
            recv_sem=sum_recv.at[phase], device_id=peers[0], device_id_type=MESH_ID,
        )

    zero_absent(f0, ybuf0, zbuf0)
    zero_absent(f1, ybuf1, zbuf1)

    pl.semaphore_wait(barrier, group - 1)

    pending = []

    def start(copies):
        for cond, out, _ in copies:
            guarded(cond, out.start)
        pending.extend(copies)

    def land(copies):
        for cond, _, arrive in copies:
            guarded(cond, arrive.wait_recv)

    halo0 = exchange(0, f0, ysend0, ybuf0, zsend0, zbuf0)
    start(halo0)
    total0 = sum_copies(0, msg0, sums0)

    load_density.wait()

    def prepare(x, carry):
        mu = mu_s[lax.shift_right_logical(x, 3)]
        lm = lm_s[lax.shift_right_logical(x, 3)]
        m = mask_s[x]
        inertia = omega * density_s[x].astype(f32)
        base = 6.0 * mu + 2.0 * lm - inertia
        for c in range(3):
            real = base + m * imp_ref[0, c]
            imag = m * imp_ref[1, c] - DAMPING * inertia
            scale = RELAXATION / (real * real + imag * imag)
            dinv[c, x] = real * scale
            dinv[3 + c, x] = imag * scale
        return carry

    lax.fori_loop(0, cx, prepare, 0, unroll=2)

    def shift_up(v):
        return jnp.where(lane == cz - 1, 0.0, pltpu.roll(v, cz - 1, 1))

    def shift_down(v):
        return jnp.where(lane == 0, 0.0, pltpu.roll(v, 1, 1))

    def z_terms(zbuf):
        sign = jnp.where(col == 0, 0.25, -0.25)
        h = zbuf[0]
        ahead = jnp.where(xs == cx - 1, pltpu.roll(zbuf[2], cx - 1, 1), pltpu.roll(h, cz - 1, 1))
        behind = jnp.where(xs == 0, pltpu.roll(zbuf[1], cz - cx + 1, 1), pltpu.roll(h, 1, 1))
        dxh = (ahead - behind) * sign
        above = jnp.where(row == cy - 1, pltpu.roll(zbuf[4], cy - 1, 0), pltpu.roll(h, cy - 1, 0))
        below = jnp.where(row == 0, pltpu.roll(zbuf[3], 1, 0), pltpu.roll(h, 1, 0))
        dyh = (above - below) * sign

        def block(c):
            own = (lane >= c * cx) & (lane < (c + 1) * cx)
            return own | ((lane >= (c + 3) * cx) & (lane < (c + 4) * cx))

        extra = jnp.where(
            block(0),
            pltpu.roll(dxh, cz - 2 * cx, 1),
            jnp.where(
                block(1),
                pltpu.roll(dyh, cz - cx, 1),
                h + pltpu.roll(dxh, 2 * cx, 1) + pltpu.roll(dyh, cx, 1),
            ),
        )
        return mu_edge * h + lm_edge * extra

    def mean_terms(slots):
        total = jnp.sum(slots[...], 0) / jnp.float32(group * cells)
        means = [jnp.sum(jnp.where(lane1 == c, total, 0.0), 1, keepdims=True) for c in range(6)]
        result = []
        for c in range(3):
            result.append(imp_ref[0, c] * means[c] - imp_ref[1, c] * means[3 + c])
        for c in range(3):
            result.append(imp_ref[0, c] * means[3 + c] + imp_ref[1, c] * means[c])
        return [jnp.broadcast_to(r, (1, cz)) for r in result]

    def y_up(v):
        return jnp.where(row == cy - 1, 0.0, pltpu.roll(v, cy - 1, 0))

    def y_down(v):
        return jnp.where(row == 0, 0.0, pltpu.roll(v, 1, 0))

    def halo_slopes(field):
        def step(k, carry):
            px = k * (cx + 1)
            for part in (0, 3):
                uy = field[part + 1, px]
                uz = field[part + 2, px]
                slope_s[part // 3, px] = y_up(uy) - y_down(uy) + (shift_up(uz) - shift_down(uz))
            return carry

        lax.fori_loop(0, 2, step, 0)

    def stencil(field, x):
        px = x + 1
        block_x = lax.shift_right_logical(x, 3)
        mu = mu_s[block_x]
        lm = lm_s[block_x]
        quarter = 0.25 * lm
        for part in (0, 3):
            mid = [field[part + c, px] for c in range(3)]
            xp = [field[part + c, px + 1] for c in range(3)]
            xm = [field[part + c, px - 1] for c in range(3)]
            yp = [y_up(v) for v in mid]
            ym = [y_down(v) for v in mid]
            zp = [shift_up(v) for v in mid]
            zm = [shift_down(v) for v in mid]
            sx = [a + b for a, b in zip(xp, xm)]
            sy = [a + b for a, b in zip(yp, ym)]
            sz = [a + b for a, b in zip(zp, zm)]
            dx0 = xp[0] - xm[0]
            dy1 = yp[1] - ym[1]
            dz2 = zp[2] - zm[2]
            slope_s[part // 3, px] = dy1 + dz2
            by_y = dx0 + dz2
            by_z = dx0 + dy1
            own = [
                lm * sx[0],
                lm * sy[1] + quarter * (y_up(by_y) - y_down(by_y)),
                lm * sz[2] + quarter * (shift_up(by_z) - shift_down(by_z)),
            ]
            for c in range(3):
                s = source_s[part + c, x].astype(f32) + own[c]
                part_s[part + c, x] = s + mu * (sx[c] + sy[c] + sz[c])

    def y_terms(ybuf):
        for side, edge_rows, sign in ((0, pl.ds(0, 8), -0.25), (1, pl.ds(cy - 8, 8), 0.25)):
            mu = jnp.concatenate([mu_s[bx, edge_rows, :] for bx in range(cx // 8)], 0)
            lm = jnp.concatenate([lm_s[bx, edge_rows, :] for bx in range(cx // 8)], 0)
            scaled = lm * sign
            for part in (0, 3):
                h = [ybuf[side, part + c, pl.ds(TOP, cx), :] for c in range(3)]
                dx = [
                    ybuf[side, part + c, pl.ds(TOP + 1, cx), :]
                    - ybuf[side, part + c, pl.ds(TOP - 1, cx), :]
                    for c in range(2)
                ]
                dz = [shift_up(h[c]) - shift_down(h[c]) for c in (1, 2)]
                ky_s[side, part] = mu * h[0] + scaled * dx[1]
                ky_s[side, part + 1] = (mu + lm) * h[1] + scaled * (dx[0] + dz[1])
                ky_s[side, part + 2] = mu * h[2] + scaled * dz[0]

    def finish(field, x, zk, zm):
        px = x + 1
        m = mask_s[x]
        quarter = 0.25 * lm_s[lax.shift_right_logical(x, 3)]
        sums = []
        for c in range(6):
            beyond = pltpu.roll(zk, (edge - (c * cx + x)) & (cz - 1), 1)
            s = part_s[c, x] + jnp.where(lane == edge, beyond, 0.0)
            low = ky_s[0, c, pl.ds(x, 1), :]
            high = ky_s[1, c, pl.ds(x, 1), :]
            s = s + jnp.where(row == 0, low, jnp.where(row == cy - 1, high, 0.0))
            if c % 3 == 0:
                s = s + quarter * (slope_s[c // 3, px + 1] - slope_s[c // 3, px - 1])
            sums.append(s + m * zm[c])
        result = [None] * 6
        for c in range(3):
            dr = dinv[c, x]
            di = dinv[3 + c, x]
            re, im = sums[c], sums[3 + c]
            result[c] = (1.0 - RELAXATION) * field[c, px] + (re * dr + im * di)
            result[3 + c] = (1.0 - RELAXATION) * field[3 + c, px] + (im * dr - re * di)
        return result, m

    def inner(field):
        def step(x, carry):
            stencil(field, x)
            return carry

        lax.fori_loop(1, cx - 1, step, 0, unroll=2)

    def outer(field):
        def step(k, carry):
            stencil(field, k * (cx - 1))
            return carry

        lax.fori_loop(0, 2, step, 0)
        halo_slopes(field)

    load_source.wait()
    inner(f0)
    land(halo0)
    outer(f0)
    y_terms(ybuf0)
    zk0 = z_terms(zbuf0)
    total0.wait_recv()
    zm0 = mean_terms(sums0)

    def sweep_one(x, carry):
        packed, accs = carry
        new, m = finish(f0, x, zk0, zm0)
        grown = []
        for c in range(6):
            f1[c, x + 1] = new[c]
            ysend1[0, c, pl.ds(x, 1), :] = new[c][:1]
            ysend1[1, c, pl.ds(x, 1), :] = new[c][cy - 1 :]
            grown.append(accs[c] + fold(m * new[c]))
            packed = pack(packed, new[c], c, x)
        return packed, tuple(grown)

    packed, accs = lax.fori_loop(
        0, cx, sweep_one, (jnp.zeros((cy, cz), f32), zero_acc), unroll=2
    )
    zsend1[...] = packed
    halo1 = exchange(1, f1, ysend1, ybuf1, zsend1, zbuf1)
    start(halo1)
    msg1[...] = to_row(accs)
    total1 = sum_copies(1, msg1, sums1)

    inner(f1)
    load_forward.wait()
    land(halo1)
    outer(f1)
    y_terms(ybuf1)
    zk1 = z_terms(zbuf1)
    total1.wait_recv()
    zm1 = mean_terms(sums1)

    def sweep_two(x, corr):
        new, _ = finish(f1, x, zk1, zm1)
        for c in range(6):
            out_ref[c, x] = new[c]
        for c in range(3):
            fr = forward_s[c, x].astype(f32)
            fi = forward_s[3 + c, x].astype(f32)
            corr = corr + (new[c] * (fr - DAMPING * fi) - new[3 + c] * (fi + DAMPING * fr))
        return corr

    bands = [
        lax.fori_loop(4 * a, 4 * a + 4, sweep_two, jnp.zeros((cy, cz), f32), unroll=2) for a in range(cx // 4)
    ]
    tall = jnp.concatenate(bands, 0)
    n_rows = tall.shape[0]
    band_sums = jnp.sum(tall, 1, keepdims=True) * (-omega / 64.0)
    spots = lax.broadcasted_iota(jnp.int32, (n_rows, cz), 1) == (
        lax.shift_right_logical(lax.broadcasted_iota(jnp.int32, (n_rows, cz), 0), 2) + gy * (n_rows // 4)
    )
    msg2[...] = jnp.sum(jnp.where(spots, band_sums, 0.0), 0, keepdims=True)
    total2 = sum_copies(2, msg2, sums2)
    per_x, per_y = cx // 4, cy // 4
    assert per_x == 4 and per_y == 4 and cx == 16 and cz == 128 and n_col == 2
    shape = (n_gx * per_x, cz)
    lanes = lax.broadcasted_iota(jnp.int32, shape, 1)
    rows_out = lax.broadcasted_iota(jnp.int32, shape, 0)
    keep = (lax.shift_right_logical(lanes, 2) & (per_x - 1)) == (rows_out & (per_x - 1))
    pick_shape = (n_gy * per_y, cz)
    target = lax.broadcasted_iota(jnp.int32, pick_shape, 0)
    origin = lax.broadcasted_iota(jnp.int32, pick_shape, 1)
    place = lax.shift_right_logical(origin, 4) * per_y + (origin & (per_y - 1))
    pick = jnp.where(place == target, 1.0, 0.0)
    total2.wait_recv()
    wide = jnp.zeros(shape, f32)
    for g in range(n_gx):
        strip = sums2[g * n_gy * n_col]
        for k in range(1, n_gy * n_col):
            strip = strip + sums2[g * n_gy * n_col + k]
        wide = jnp.where((rows_out >= g * per_x) & (rows_out < (g + 1) * per_x), strip, wide)
    wide = jnp.where(keep, wide, 0.0)
    coarse_ref[...] = lax.dot_general(
        pick, wide, (((1,), (1,)), ((), ())),
        preferred_element_type=f32, precision=lax.Precision.HIGHEST,
    )
    for cond, out, _ in pending:
        guarded(cond, out.wait_send)
    for total in (total0, total1, total2):
        total.wait_send()


def shards(n_gx, n_gy, n_col, source, warm, forward, density, material_map, material_table,
           iface_cells, impedance, omega2):
    f32 = jnp.float32
    cx, cy, cz = density.shape
    group = n_gx * n_gy * n_col
    vmem = pl.BlockSpec(memory_space=pltpu.VMEM)
    smem = pl.BlockSpec(memory_space=pltpu.SMEM)
    hbm = pl.BlockSpec(memory_space=pltpu.HBM)
    field = pltpu.VMEM((6, cx + 2, cy, cz), f32)
    tile = (cx, cy, cz)
    y_halo = pltpu.VMEM((2, 6, TOP + cx + 8, cz), f32)
    y_face = pltpu.VMEM((2, 6, cx, cz), f32)
    table = material_table.T
    warm, source, density, forward, iface_cells, material_map, table, impedance = (
        pltpu.with_memory_space_constraint(a, pltpu.HBM)
        for a in (warm, source, density, forward, iface_cells, material_map, table, impedance)
    )
    adjoint, coarse = pl.pallas_call(
        functools.partial(kernel, n_gx, n_gy, n_col),
        out_shape=(
            jax.ShapeDtypeStruct((6,) + tile, f32),
            jax.ShapeDtypeStruct((n_gy * (cy // 4), n_gx * (cx // 4)), f32),
        ),
        in_specs=[hbm, hbm, hbm, hbm, vmem, smem, smem, smem, smem],
        out_specs=(vmem, vmem),
        scratch_shapes=[
            field, field,
            pltpu.VMEM((5, cy, cz), f32), pltpu.VMEM((5, cy, cz), f32),
            pltpu.VMEM((cy, cz), f32), pltpu.VMEM((cy, cz), f32),
            y_halo, y_halo, y_face, y_face,
            pltpu.VMEM((group, 1, cz), f32), pltpu.VMEM((group, 1, cz), f32),
            pltpu.VMEM((group, 1, cz), f32),
            pltpu.VMEM((1, cz), f32), pltpu.VMEM((1, cz), f32), pltpu.VMEM((1, cz), f32),
            pltpu.VMEM(tile, f32),
            pltpu.VMEM((cx // 8, cy, cz), f32), pltpu.VMEM((cx // 8, cy, cz), f32),
            pltpu.VMEM((6,) + tile, f32),
            pltpu.VMEM((6,) + tile, jnp.bfloat16),
            pltpu.VMEM((6,) + tile, jnp.bfloat16),
            pltpu.VMEM(tile, jnp.bfloat16),
            pltpu.VMEM((6,) + tile, jnp.bfloat16),
            pltpu.VMEM((6,) + tile, f32),
            y_face,
            pltpu.VMEM((2, cx + 2, cy, cz), f32),
            pltpu.SemaphoreType.DMA((4,)),
            pltpu.SemaphoreType.DMA((2, 13)),
            pltpu.SemaphoreType.DMA((2, 13)),
            pltpu.SemaphoreType.DMA((3,)),
            pltpu.SemaphoreType.DMA((3,)),
        ],
        compiler_params=pltpu.CompilerParams(
            collective_id=0, has_side_effects=True, vmem_limit_bytes=32 * 1024 * 1024
        ),
        name="adjoint_sweeps",
    )(warm, source, density, forward, iface_cells, material_map, table, impedance, omega2)
    return adjoint, coarse.T


def solution(mesh):
    in_specs = (
        P("freq", "gx", "gy", "col"),
        P("freq", "gx", "gy", "col"),
        P("freq", "gx", "gy", "col"),
        P("gx", "gy", "col"),
        P("gx", "gy", "col"),
        P(),
        P(("gx", "gy", "col"), None),
        P(),
        P("freq"),
    )
    out_specs = (P("freq", "gx", "gy", "col"), P("freq", None))
    body = functools.partial(shards, mesh.shape["gx"], mesh.shape["gy"], mesh.shape["col"])
    return jax.shard_map(body, mesh=mesh, in_specs=in_specs, out_specs=out_specs, check_vma=False)
```

```python
import functools
import jax
import jax.numpy as jnp
from jax import lax
from jax.experimental import pallas as pl
from jax.experimental.pallas import tpu as pltpu
from jax.sharding import PartitionSpec as P

DAMPING = 0.5
RELAXATION = 0.6
MESH_ID = pl.DeviceIdType.MESH
TOP = 8


def kernel(
    n_gx, n_gy, n_col,
    warm_hbm, source_hbm, density_hbm, forward_hbm, cells_ref,
    map_ref, table_ref, imp_ref, omega_ref,
    out_ref, coarse_ref,
    f0, f1, zbuf0, zbuf1, zsend0, zsend1, ybuf0, ybuf1, ysend0, ysend1,
    xhalf0, xhalf1, xsend, yhalf0, yhalf1, ysend_half0, ysend_half1,
    sums0, sums1, sums2, msg0, msg1, msg2,
    mask_s, mu_s, lm_s, dinv, warm_s, source_s, density_s, forward_s, part_s, ky_s, slope_s,
    local_sem, halo_send, halo_recv, sum_send, sum_recv,
):
    f32 = jnp.float32
    cx, cy, cz = warm_hbm.shape[1:]
    cells = cells_ref.shape[1]
    group = n_gx * n_gy * n_col
    gx = lax.axis_index("gx")
    gy = lax.axis_index("gy")
    col = lax.axis_index("col")
    me = (gx * n_gy + gy) * n_col + col

    def turned(position, length):
        steps = [position + d for d in range(length)]
        return [steps[0]] + [jnp.where(t >= length, t - length, t) for t in steps[1:]]

    peers = []
    for other_gx in turned(gx, n_gx):
        for other_gy in turned(gy, n_gy):
            for other_col in turned(col, n_col):
                peers.append({"gx": other_gx, "gy": other_gy, "col": other_col})
    peers = peers[1:]

    barrier = pltpu.get_barrier_semaphore()
    for other in peers:
        pl.semaphore_signal(barrier, inc=1, device_id=other, device_id_type=MESH_ID)

    load_density = pltpu.make_async_copy(density_hbm, density_s, local_sem.at[0])
    load_source = pltpu.make_async_copy(source_hbm, source_s, local_sem.at[1])
    load_forward = pltpu.make_async_copy(forward_hbm, forward_s, local_sem.at[2])
    load_warm = pltpu.make_async_copy(warm_hbm, warm_s, local_sem.at[3])
    load_warm.start()
    load_density.start()
    load_source.start()
    load_forward.start()

    lane = lax.broadcasted_iota(jnp.int32, (cy, cz), 1)
    row = lax.broadcasted_iota(jnp.int32, (cy, cz), 0)
    lane1 = lax.broadcasted_iota(jnp.int32, (1, cz), 1)
    edge = jnp.where(col == 0, cz - 1, 0)
    omega = omega_ref[0]

    idx = cells_ref[...]
    hot_row = jnp.where(
        lax.broadcasted_iota(jnp.int32, (cx * cy, cells), 0) == lax.shift_right_logical(idx, cz.bit_length() - 1), 1.0, 0.0
    ).astype(jnp.bfloat16)
    hot_lane = jnp.where(
        lax.broadcasted_iota(jnp.int32, (cz, cells), 0) == (idx & (cz - 1)), 1.0, 0.0
    ).astype(jnp.bfloat16)
    mask = lax.dot_general(
        hot_row, hot_lane, (((1,), (1,)), ((), ())), preferred_element_type=f32
    )
    mask_s[...] = mask.reshape(cx, cy, cz)

    def pack(packed, value, c, x):
        spot = c * cx + x
        moved = pltpu.roll(value, (spot - edge) & (cz - 1), 1)
        return jnp.where(lane == spot, moved, packed)

    def fold(value):
        return value[:8] + value[8:]

    def to_row(accs):
        tall = jnp.concatenate([jnp.sum(a, 0, keepdims=True) for a in accs] + [jnp.zeros((2, cz), f32)], 0)
        total = jnp.sum(tall, 1, keepdims=True)
        spots = lax.broadcasted_iota(jnp.int32, (8, cz), 0) == lax.broadcasted_iota(jnp.int32, (8, cz), 1)
        return jnp.sum(jnp.where(spots, total, 0.0), 0, keepdims=True)

    zero_acc = tuple(jnp.zeros((8, cz), f32) for _ in range(6))

    def convert(x, carry):
        packed, accs = carry
        m = mask_s[x]
        grown = []
        for c in range(6):
            v = warm_s[c, x].astype(f32)
            f0[c, x + 1] = v
            ysend0[0, c, pl.ds(x, 1), :] = v[:1]
            ysend0[1, c, pl.ds(x, 1), :] = v[cy - 1 :]
            grown.append(accs[c] + fold(m * v))
            packed = pack(packed, v, c, x)
        return packed, tuple(grown)


    load_warm.wait()
    packed, accs = lax.fori_loop(0, cx, convert, (jnp.zeros((cy, cz), f32), zero_acc), unroll=2)
    zsend0[...] = packed.astype(jnp.bfloat16)
    ysend_half0[...] = ysend0[...].astype(jnp.bfloat16)
    msg0[...] = to_row(accs)

    has = {"xm": gx > 0, "xp": gx < n_gx - 1, "ym": gy > 0, "yp": gy < n_gy - 1}

    def both(a, b):
        return jnp.logical_and(has[a], has[b])

    sources = [
        (has["xm"], -1, 0, False), (has["xp"], 1, 0, False),
        (has["ym"], 0, -1, False), (has["yp"], 0, 1, False),
        (both("xm", "ym"), -1, -1, False), (both("xm", "yp"), -1, 1, False),
        (both("xp", "ym"), 1, -1, False), (both("xp", "yp"), 1, 1, False),
        (None, 0, 0, True),
        (has["xm"], -1, 0, True), (has["xp"], 1, 0, True),
        (has["ym"], 0, -1, True), (has["yp"], 0, 1, True),
    ]

    def face(xfaces, ysend, ysend_half, dx, dy):
        if dy == 0:
            return xfaces[0 if dx < 0 else 1]
        side = 0 if dy < 0 else 1
        if dx == 0:
            return ysend_half.at[side]
        return ysend.at[side, :, pl.ds(0 if dx < 0 else cx - 1, 1), :]

    def halo(xhalf, ybuf, yhalf, dx, dy):
        if dy == 0:
            return xhalf.at[0 if dx < 0 else 1]
        side = 0 if dy < 0 else 1
        if dx == 0:
            return yhalf.at[side]
        return ybuf.at[side, :, pl.ds(TOP - 1 if dx < 0 else TOP + cx, 1), :]

    def exchange(phase, xfaces, xhalf, ysend, ysend_half, ybuf, yhalf, zsend, zbuf):
        result = []
        for k, (cond, dx, dy, flip) in enumerate(sources):
            opposite = next(
                j for j, s in enumerate(sources) if s[1] == -dx and s[2] == -dy and s[3] == flip
            )
            if flip:
                src = zsend
                dst = zbuf.at[opposite - 8]
                here = zbuf.at[k - 8]
            else:
                src = face(xfaces, ysend, ysend_half, dx, dy)
                dst = halo(xhalf, ybuf, yhalf, -dx, -dy)
                here = halo(xhalf, ybuf, yhalf, dx, dy)
            target = {"gx": gx + dx, "gy": gy + dy, "col": 1 - col if flip else col}
            out = pltpu.make_async_remote_copy(
                src_ref=src, dst_ref=dst, send_sem=halo_send.at[phase, k],
                recv_sem=halo_recv.at[phase, opposite], device_id=target, device_id_type=MESH_ID,
            )
            arrive = pltpu.make_async_remote_copy(
                src_ref=here, dst_ref=here, send_sem=halo_send.at[phase, k],
                recv_sem=halo_recv.at[phase, k], device_id=target, device_id_type=MESH_ID,
            )
            result.append((cond, out, arrive))
        return result

    def guarded(cond, action):
        if cond is None:
            action()
        else:
            pl.when(cond)(action)

    def zero_absent(xhalf, ybuf, yhalf, zbuf):
        for k, (cond, dx, dy, flip) in enumerate(sources):
            if cond is None:
                continue

            def clear(k=k, dx=dx, dy=dy, flip=flip):
                if flip:
                    zbuf[k - 8] = jnp.zeros(zbuf.shape[1:], zbuf.dtype)
                else:
                    part = halo(xhalf, ybuf, yhalf, dx, dy)
                    part[...] = jnp.zeros(part.shape, part.dtype)

            pl.when(jnp.logical_not(cond))(clear)

    def sum_copies(phase, msg, slots):
        for other in peers:
            pltpu.make_async_remote_copy(
                src_ref=msg, dst_ref=slots.at[me], send_sem=sum_send.at[phase],
                recv_sem=sum_recv.at[phase], device_id=other, device_id_type=MESH_ID,
            ).start()
        slots[me] = msg[...]
        rest = slots.at[pl.ds(0, group - 1)]
        return pltpu.make_async_remote_copy(
            src_ref=rest, dst_ref=rest, send_sem=sum_send.at[phase],
            recv_sem=sum_recv.at[phase], device_id=peers[0], device_id_type=MESH_ID,
        )

    zero_absent(xhalf0, ybuf0, yhalf0, zbuf0)
    zero_absent(xhalf1, ybuf1, yhalf1, zbuf1)

    pl.semaphore_wait(barrier, group - 1)

    pending = []

    def start(copies):
        for cond, out, _ in copies:
            guarded(cond, out.start)
        pending.extend(copies)

    def land(copies):
        for cond, _, arrive in copies:
            guarded(cond, arrive.wait_recv)

    halo0 = exchange(
        0, (warm_s.at[:, 0], warm_s.at[:, cx - 1]), xhalf0,
        ysend0, ysend_half0, ybuf0, yhalf0, zsend0, zbuf0,
    )
    start(halo0)
    total0 = sum_copies(0, msg0, sums0)

    blocks = map_ref.shape
    for bx in range(blocks[0]):
        mus = []
        lms = []
        for by in range(blocks[1]):
            mu = jnp.zeros((8, cz), f32)
            lm = jnp.zeros((8, cz), f32)
            for bz in range(blocks[2]):
                entry = map_ref[bx, by, bz]
                here = (lane[:8] >= 32 * bz) & (lane[:8] < 32 * (bz + 1))
                lm = jnp.where(here, table_ref[0, entry], lm)
                mu = jnp.where(here, table_ref[1, entry], mu)
            mus.append(mu)
            lms.append(lm + mu)
        mu_s[bx] = jnp.concatenate(mus, 0)
        lm_s[bx] = jnp.concatenate(lms, 0)
    xs = lane & (cx - 1)
    mu_edge = jnp.zeros((cy, cz), f32)
    lm_edge = jnp.zeros((cy, cz), f32)
    edge_block = jnp.where(col == 0, blocks[2] - 1, 0)
    for bx in range(blocks[0]):
        for by in range(blocks[1]):
            entry = map_ref[bx, by, edge_block]
            here = ((xs >= 8 * bx) & (xs < 8 * (bx + 1))) & ((row >= 8 * by) & (row < 8 * (by + 1)))
            mu_edge = jnp.where(here, table_ref[1, entry], mu_edge)
            lm_edge = jnp.where(here, table_ref[0, entry] + table_ref[1, entry], lm_edge)

    load_density.wait()

    def prepare(x, carry):
        mu = mu_s[lax.shift_right_logical(x, 3)]
        lm = lm_s[lax.shift_right_logical(x, 3)]
        m = mask_s[x]
        inertia = omega * density_s[x].astype(f32)
        base = 6.0 * mu + 2.0 * lm - inertia
        for c in range(3):
            real = base + m * imp_ref[0, c]
            imag = m * imp_ref[1, c] - DAMPING * inertia
            scale = RELAXATION / (real * real + imag * imag)
            dinv[c, x] = real * scale
            dinv[3 + c, x] = imag * scale
        return carry

    lax.fori_loop(0, cx, prepare, 0, unroll=2)

    def shift_up(v):
        return jnp.where(lane == cz - 1, 0.0, pltpu.roll(v, cz - 1, 1))

    def shift_down(v):
        return jnp.where(lane == 0, 0.0, pltpu.roll(v, 1, 1))

    def z_terms(zbuf):
        sign = jnp.where(col == 0, 0.25, -0.25)
        h, before, after, under, over = (zbuf[k].astype(f32) for k in range(5))
        ahead = jnp.where(xs == cx - 1, pltpu.roll(after, cx - 1, 1), pltpu.roll(h, cz - 1, 1))
        behind = jnp.where(xs == 0, pltpu.roll(before, cz - cx + 1, 1), pltpu.roll(h, 1, 1))
        dxh = (ahead - behind) * sign
        above = jnp.where(row == cy - 1, pltpu.roll(over, cy - 1, 0), pltpu.roll(h, cy - 1, 0))
        below = jnp.where(row == 0, pltpu.roll(under, 1, 0), pltpu.roll(h, 1, 0))
        dyh = (above - below) * sign

        def block(c):
            own = (lane >= c * cx) & (lane < (c + 1) * cx)
            return own | ((lane >= (c + 3) * cx) & (lane < (c + 4) * cx))

        extra = jnp.where(
            block(0),
            pltpu.roll(dxh, cz - 2 * cx, 1),
            jnp.where(
                block(1),
                pltpu.roll(dyh, cz - cx, 1),
                h + pltpu.roll(dxh, 2 * cx, 1) + pltpu.roll(dyh, cx, 1),
            ),
        )
        return mu_edge * h + lm_edge * extra

    def mean_terms(slots):
        total = jnp.sum(slots[...], 0) / jnp.float32(group * cells)
        means = [jnp.sum(jnp.where(lane1 == c, total, 0.0), 1, keepdims=True) for c in range(6)]
        result = []
        for c in range(3):
            result.append(imp_ref[0, c] * means[c] - imp_ref[1, c] * means[3 + c])
        for c in range(3):
            result.append(imp_ref[0, c] * means[3 + c] + imp_ref[1, c] * means[c])
        return [jnp.broadcast_to(r, (1, cz)) for r in result]

    def y_up(v):
        return jnp.where(row == cy - 1, 0.0, pltpu.roll(v, cy - 1, 0))

    def y_down(v):
        return jnp.where(row == 0, 0.0, pltpu.roll(v, 1, 0))

    def halo_slopes(field):
        def step(k, carry):
            px = k * (cx + 1)
            for part in (0, 3):
                uy = field[part + 1, px]
                uz = field[part + 2, px]
                slope_s[part // 3, px] = y_up(uy) - y_down(uy) + (shift_up(uz) - shift_down(uz))
            return carry

        lax.fori_loop(0, 2, step, 0)

    def stencil(field, x):
        px = x + 1
        block_x = lax.shift_right_logical(x, 3)
        mu = mu_s[block_x]
        lm = lm_s[block_x]
        quarter = 0.25 * lm
        for part in (0, 3):
            mid = [field[part + c, px] for c in range(3)]
            xp = [field[part + c, px + 1] for c in range(3)]
            xm = [field[part + c, px - 1] for c in range(3)]
            yp = [y_up(v) for v in mid]
            ym = [y_down(v) for v in mid]
            zp = [shift_up(v) for v in mid]
            zm = [shift_down(v) for v in mid]
            sx = [a + b for a, b in zip(xp, xm)]
            sy = [a + b for a, b in zip(yp, ym)]
            sz = [a + b for a, b in zip(zp, zm)]
            dx0 = xp[0] - xm[0]
            dy1 = yp[1] - ym[1]
            dz2 = zp[2] - zm[2]
            slope_s[part // 3, px] = dy1 + dz2
            by_y = dx0 + dz2
            by_z = dx0 + dy1
            own = [
                lm * sx[0],
                lm * sy[1] + quarter * (y_up(by_y) - y_down(by_y)),
                lm * sz[2] + quarter * (shift_up(by_z) - shift_down(by_z)),
            ]
            for c in range(3):
                s = source_s[part + c, x].astype(f32) + own[c]
                part_s[part + c, x] = s + mu * (sx[c] + sy[c] + sz[c])

    def y_terms(ybuf, yhalf):
        ybuf[:, :, pl.ds(TOP, cx), :] = yhalf[...].astype(f32)
        for side, edge_rows, sign in ((0, pl.ds(0, 8), -0.25), (1, pl.ds(cy - 8, 8), 0.25)):
            mu = jnp.concatenate([mu_s[bx, edge_rows, :] for bx in range(cx // 8)], 0)
            lm = jnp.concatenate([lm_s[bx, edge_rows, :] for bx in range(cx // 8)], 0)
            scaled = lm * sign
            for part in (0, 3):
                h = [ybuf[side, part + c, pl.ds(TOP, cx), :] for c in range(3)]
                dx = [
                    ybuf[side, part + c, pl.ds(TOP + 1, cx), :]
                    - ybuf[side, part + c, pl.ds(TOP - 1, cx), :]
                    for c in range(2)
                ]
                dz = [shift_up(h[c]) - shift_down(h[c]) for c in (1, 2)]
                ky_s[side, part] = mu * h[0] + scaled * dx[1]
                ky_s[side, part + 1] = (mu + lm) * h[1] + scaled * (dx[0] + dz[1])
                ky_s[side, part + 2] = mu * h[2] + scaled * dz[0]

    def finish(field, x, zk, zm):
        px = x + 1
        m = mask_s[x]
        quarter = 0.25 * lm_s[lax.shift_right_logical(x, 3)]
        sums = []
        for c in range(6):
            beyond = pltpu.roll(zk, (edge - (c * cx + x)) & (cz - 1), 1)
            s = part_s[c, x] + jnp.where(lane == edge, beyond, 0.0)
            low = ky_s[0, c, pl.ds(x, 1), :]
            high = ky_s[1, c, pl.ds(x, 1), :]
            s = s + jnp.where(row == 0, low, jnp.where(row == cy - 1, high, 0.0))
            if c % 3 == 0:
                s = s + quarter * (slope_s[c // 3, px + 1] - slope_s[c // 3, px - 1])
            sums.append(s + m * zm[c])
        result = [None] * 6
        for c in range(3):
            dr = dinv[c, x]
            di = dinv[3 + c, x]
            re, im = sums[c], sums[3 + c]
            result[c] = (1.0 - RELAXATION) * field[c, px] + (re * dr + im * di)
            result[3 + c] = (1.0 - RELAXATION) * field[3 + c, px] + (im * dr - re * di)
        return result, m

    def inner(field):
        def step(x, carry):
            stencil(field, x)
            return carry

        lax.fori_loop(1, cx - 1, step, 0, unroll=2)

    def outer(field, xhalf):
        field[:, 0] = xhalf[0].astype(f32)
        field[:, cx + 1] = xhalf[1].astype(f32)

        def step(k, carry):
            stencil(field, k * (cx - 1))
            return carry

        lax.fori_loop(0, 2, step, 0)
        halo_slopes(field)

    load_source.wait()
    inner(f0)
    land(halo0)
    outer(f0, xhalf0)
    y_terms(ybuf0, yhalf0)
    zk0 = z_terms(zbuf0)
    total0.wait_recv()
    zm0 = mean_terms(sums0)

    def sweep_one(x, carry):
        packed, accs = carry
        new, m = finish(f0, x, zk0, zm0)
        grown = []
        for c in range(6):
            f1[c, x + 1] = new[c]
            ysend1[0, c, pl.ds(x, 1), :] = new[c][:1]
            ysend1[1, c, pl.ds(x, 1), :] = new[c][cy - 1 :]
            grown.append(accs[c] + fold(m * new[c]))
            packed = pack(packed, new[c], c, x)
        return packed, tuple(grown)

    packed, accs = lax.fori_loop(
        0, cx, sweep_one, (jnp.zeros((cy, cz), f32), zero_acc), unroll=2
    )
    zsend1[...] = packed.astype(jnp.bfloat16)
    ysend_half1[...] = ysend1[...].astype(jnp.bfloat16)
    xsend[0] = f1[:, 1].astype(jnp.bfloat16)
    xsend[1] = f1[:, cx].astype(jnp.bfloat16)
    halo1 = exchange(
        1, (xsend.at[0], xsend.at[1]), xhalf1,
        ysend1, ysend_half1, ybuf1, yhalf1, zsend1, zbuf1,
    )
    start(halo1)
    msg1[...] = to_row(accs)
    total1 = sum_copies(1, msg1, sums1)

    inner(f1)
    load_forward.wait()
    land(halo1)
    outer(f1, xhalf1)
    y_terms(ybuf1, yhalf1)
    zk1 = z_terms(zbuf1)
    total1.wait_recv()
    zm1 = mean_terms(sums1)

    def sweep_two(x, corr):
        new, _ = finish(f1, x, zk1, zm1)
        for c in range(6):
            out_ref[c, x] = new[c]
        for c in range(3):
            fr = forward_s[c, x].astype(f32)
            fi = forward_s[3 + c, x].astype(f32)
            corr = corr + (new[c] * (fr - DAMPING * fi) - new[3 + c] * (fi + DAMPING * fr))
        return corr

    bands = [
        lax.fori_loop(4 * a, 4 * a + 4, sweep_two, jnp.zeros((cy, cz), f32), unroll=2) for a in range(cx // 4)
    ]
    tall = jnp.concatenate(bands, 0)
    n_rows = tall.shape[0]
    band_sums = jnp.sum(tall, 1, keepdims=True) * (-omega / 64.0)
    spots = lax.broadcasted_iota(jnp.int32, (n_rows, cz), 1) == (
        lax.shift_right_logical(lax.broadcasted_iota(jnp.int32, (n_rows, cz), 0), 2) + gy * (n_rows // 4)
    )
    msg2[...] = jnp.sum(jnp.where(spots, band_sums, 0.0), 0, keepdims=True)
    total2 = sum_copies(2, msg2, sums2)
    per_x, per_y = cx // 4, cy // 4
    assert per_x == 4 and per_y == 4 and cx == 16 and cz == 128 and n_col == 2
    shape = (n_gx * per_x, cz)
    lanes = lax.broadcasted_iota(jnp.int32, shape, 1)
    rows_out = lax.broadcasted_iota(jnp.int32, shape, 0)
    keep = (lax.shift_right_logical(lanes, 2) & (per_x - 1)) == (rows_out & (per_x - 1))
    pick_shape = (n_gy * per_y, cz)
    target = lax.broadcasted_iota(jnp.int32, pick_shape, 0)
    origin = lax.broadcasted_iota(jnp.int32, pick_shape, 1)
    place = lax.shift_right_logical(origin, 4) * per_y + (origin & (per_y - 1))
    pick = jnp.where(place == target, 1.0, 0.0)
    total2.wait_recv()
    wide = jnp.zeros(shape, f32)
    for g in range(n_gx):
        strip = sums2[g * n_gy * n_col]
        for k in range(1, n_gy * n_col):
            strip = strip + sums2[g * n_gy * n_col + k]
        wide = jnp.where((rows_out >= g * per_x) & (rows_out < (g + 1) * per_x), strip, wide)
    wide = jnp.where(keep, wide, 0.0)
    coarse_ref[...] = lax.dot_general(
        pick, wide, (((1,), (1,)), ((), ())),
        preferred_element_type=f32, precision=lax.Precision.HIGHEST,
    )
    for cond, out, _ in pending:
        guarded(cond, out.wait_send)
    for total in (total0, total1, total2):
        total.wait_send()


def shards(n_gx, n_gy, n_col, source, warm, forward, density, material_map, material_table,
           iface_cells, impedance, omega2):
    f32 = jnp.float32
    cx, cy, cz = density.shape
    group = n_gx * n_gy * n_col
    vmem = pl.BlockSpec(memory_space=pltpu.VMEM)
    smem = pl.BlockSpec(memory_space=pltpu.SMEM)
    hbm = pl.BlockSpec(memory_space=pltpu.HBM)
    field = pltpu.VMEM((6, cx + 2, cy, cz), f32)
    tile = (cx, cy, cz)
    y_halo = pltpu.VMEM((2, 6, TOP + cx + 8, cz), f32)
    y_face = pltpu.VMEM((2, 6, cx, cz), f32)
    half = pltpu.VMEM((2, 6, 16, cz), jnp.bfloat16)
    table = material_table.T
    warm, source, density, forward, iface_cells, material_map, table, impedance = (
        pltpu.with_memory_space_constraint(a, pltpu.HBM)
        for a in (warm, source, density, forward, iface_cells, material_map, table, impedance)
    )
    adjoint, coarse = pl.pallas_call(
        functools.partial(kernel, n_gx, n_gy, n_col),
        out_shape=(
            jax.ShapeDtypeStruct((6,) + tile, f32),
            jax.ShapeDtypeStruct((n_gy * (cy // 4), n_gx * (cx // 4)), f32),
        ),
        in_specs=[hbm, hbm, hbm, hbm, vmem, smem, smem, smem, smem],
        out_specs=(vmem, vmem),
        scratch_shapes=[
            field, field,
            pltpu.VMEM((5, cy, cz), jnp.bfloat16), pltpu.VMEM((5, cy, cz), jnp.bfloat16),
            pltpu.VMEM((cy, cz), jnp.bfloat16), pltpu.VMEM((cy, cz), jnp.bfloat16),
            y_halo, y_halo, y_face, y_face,
            half, half, half, half, half, half, half,
            pltpu.VMEM((group, 1, cz), f32), pltpu.VMEM((group, 1, cz), f32),
            pltpu.VMEM((group, 1, cz), f32),
            pltpu.VMEM((1, cz), f32), pltpu.VMEM((1, cz), f32), pltpu.VMEM((1, cz), f32),
            pltpu.VMEM(tile, f32),
            pltpu.VMEM((cx // 8, cy, cz), f32), pltpu.VMEM((cx // 8, cy, cz), f32),
            pltpu.VMEM((6,) + tile, f32),
            pltpu.VMEM((6,) + tile, jnp.bfloat16),
            pltpu.VMEM((6,) + tile, jnp.bfloat16),
            pltpu.VMEM(tile, jnp.bfloat16),
            pltpu.VMEM((6,) + tile, jnp.bfloat16),
            pltpu.VMEM((6,) + tile, f32),
            y_face,
            pltpu.VMEM((2, cx + 2, cy, cz), f32),
            pltpu.SemaphoreType.DMA((4,)),
            pltpu.SemaphoreType.DMA((2, 13)),
            pltpu.SemaphoreType.DMA((2, 13)),
            pltpu.SemaphoreType.DMA((3,)),
            pltpu.SemaphoreType.DMA((3,)),
        ],
        compiler_params=pltpu.CompilerParams(
            collective_id=0, has_side_effects=True, vmem_limit_bytes=32 * 1024 * 1024
        ),
        name="adjoint_sweeps",
    )(warm, source, density, forward, iface_cells, material_map, table, impedance, omega2)
    return adjoint, coarse.T


def solution(mesh):
    in_specs = (
        P("freq", "gx", "gy", "col"),
        P("freq", "gx", "gy", "col"),
        P("freq", "gx", "gy", "col"),
        P("gx", "gy", "col"),
        P("gx", "gy", "col"),
        P(),
        P(("gx", "gy", "col"), None),
        P(),
        P("freq"),
    )
    out_specs = (P("freq", "gx", "gy", "col"), P("freq", None))
    body = functools.partial(shards, mesh.shape["gx"], mesh.shape["gy"], mesh.shape["col"])
    return jax.shard_map(body, mesh=mesh, in_specs=in_specs, out_specs=out_specs, check_vma=False)
```

```python
import functools
import jax
import jax.numpy as jnp
from jax import lax
from jax.experimental import pallas as pl
from jax.experimental.pallas import tpu as pltpu
from jax.sharding import PartitionSpec as P

DAMPING = 0.5
RELAXATION = 0.6
MESH_ID = pl.DeviceIdType.MESH
TOP = 8


def kernel(
    n_gx, n_gy, n_col,
    warm_hbm, source_hbm, density_hbm, forward_hbm, cells_ref,
    map_ref, table_ref, imp_ref, omega_ref,
    out_ref, coarse_ref,
    f0, f1, zbuf0, zbuf1, zsend0, zsend1, ybuf0, ybuf1, ysend0, ysend1,
    xhalf0, xhalf1, xsend, yhalf0, yhalf1, ysend_half0, ysend_half1,
    sums0, sums1, sums2, msg0, msg1, msg2,
    mask_s, mu_s, lm_s, dinv, warm_s, source_s, density_s, forward_s, part_s, ky_s, slope_s,
    local_sem, halo_send, halo_recv, sum_send, sum_recv,
):
    f32 = jnp.float32
    cx, cy, cz = warm_hbm.shape[1:]
    cells = cells_ref.shape[1]
    group = n_gx * n_gy * n_col
    gx = lax.axis_index("gx")
    gy = lax.axis_index("gy")
    col = lax.axis_index("col")
    me = (gx * n_gy + gy) * n_col + col

    def turned(position, length):
        steps = [position + d for d in range(length)]
        return [steps[0]] + [jnp.where(t >= length, t - length, t) for t in steps[1:]]

    peers = []
    for other_gx in turned(gx, n_gx):
        for other_gy in turned(gy, n_gy):
            for other_col in turned(col, n_col):
                peers.append({"gx": other_gx, "gy": other_gy, "col": other_col})
    peers = peers[1:]

    barrier = pltpu.get_barrier_semaphore()
    for other in peers:
        pl.semaphore_signal(barrier, inc=1, device_id=other, device_id_type=MESH_ID)

    load_density = pltpu.make_async_copy(density_hbm, density_s, local_sem.at[0])
    load_source = pltpu.make_async_copy(source_hbm, source_s, local_sem.at[1])
    load_forward = pltpu.make_async_copy(forward_hbm, forward_s, local_sem.at[2])
    load_warm = pltpu.make_async_copy(warm_hbm, warm_s, local_sem.at[3])
    load_warm.start()
    load_density.start()
    load_source.start()
    load_forward.start()

    lane = lax.broadcasted_iota(jnp.int32, (cy, cz), 1)
    row = lax.broadcasted_iota(jnp.int32, (cy, cz), 0)
    lane1 = lax.broadcasted_iota(jnp.int32, (1, cz), 1)
    edge = jnp.where(col == 0, cz - 1, 0)
    omega = omega_ref[0]

    idx = cells_ref[...]
    hot_row = jnp.where(
        lax.broadcasted_iota(jnp.int32, (cx * cy, cells), 0) == lax.shift_right_logical(idx, cz.bit_length() - 1), 1.0, 0.0
    ).astype(jnp.bfloat16)
    hot_lane = jnp.where(
        lax.broadcasted_iota(jnp.int32, (cz, cells), 0) == (idx & (cz - 1)), 1.0, 0.0
    ).astype(jnp.bfloat16)
    mask = lax.dot_general(
        hot_row, hot_lane, (((1,), (1,)), ((), ())), preferred_element_type=f32
    )
    mask_s[...] = mask.reshape(cx, cy, cz)

    def pack(packed, value, c, x):
        spot = c * cx + x
        moved = pltpu.roll(value, (spot - edge) & (cz - 1), 1)
        return jnp.where(lane == spot, moved, packed)

    def fold(value):
        return value[:8] + value[8:]

    def to_row(accs):
        tall = jnp.concatenate([jnp.sum(a, 0, keepdims=True) for a in accs] + [jnp.zeros((2, cz), f32)], 0)
        total = jnp.sum(tall, 1, keepdims=True)
        spots = lax.broadcasted_iota(jnp.int32, (8, cz), 0) == lax.broadcasted_iota(jnp.int32, (8, cz), 1)
        return jnp.sum(jnp.where(spots, total, 0.0), 0, keepdims=True)

    zero_acc = tuple(jnp.zeros((8, cz), f32) for _ in range(6))

    def convert(x, carry):
        packed, accs = carry
        m = mask_s[x]
        grown = []
        for c in range(6):
            v = warm_s[c, x].astype(f32)
            f0[c, x + 1] = v
            ysend0[0, c, pl.ds(x, 1), :] = v[:1]
            ysend0[1, c, pl.ds(x, 1), :] = v[cy - 1 :]
            grown.append(accs[c] + fold(m * v))
            packed = pack(packed, v, c, x)
        return packed, tuple(grown)


    load_warm.wait()
    packed, accs = lax.fori_loop(0, cx, convert, (jnp.zeros((cy, cz), f32), zero_acc), unroll=2)
    zsend0[...] = packed.astype(jnp.bfloat16)
    ysend_half0[...] = ysend0[...].astype(jnp.bfloat16)
    msg0[...] = to_row(accs)

    has = {"xm": gx > 0, "xp": gx < n_gx - 1, "ym": gy > 0, "yp": gy < n_gy - 1}

    def both(a, b):
        return jnp.logical_and(has[a], has[b])

    sources = [
        (has["xm"], -1, 0, False), (has["xp"], 1, 0, False),
        (has["ym"], 0, -1, False), (has["yp"], 0, 1, False),
        (both("xm", "ym"), -1, -1, False), (both("xm", "yp"), -1, 1, False),
        (both("xp", "ym"), 1, -1, False), (both("xp", "yp"), 1, 1, False),
        (None, 0, 0, True),
        (has["xm"], -1, 0, True), (has["xp"], 1, 0, True),
        (has["ym"], 0, -1, True), (has["yp"], 0, 1, True),
    ]

    def face(xfaces, ysend, ysend_half, dx, dy):
        if dy == 0:
            return xfaces[0 if dx < 0 else 1]
        side = 0 if dy < 0 else 1
        if dx == 0:
            return ysend_half.at[side]
        return ysend.at[side, :, pl.ds(0 if dx < 0 else cx - 1, 1), :]

    def halo(xhalf, ybuf, yhalf, dx, dy):
        if dy == 0:
            return xhalf.at[0 if dx < 0 else 1]
        side = 0 if dy < 0 else 1
        if dx == 0:
            return yhalf.at[side]
        return ybuf.at[side, :, pl.ds(TOP - 1 if dx < 0 else TOP + cx, 1), :]

    def exchange(phase, xfaces, xhalf, ysend, ysend_half, ybuf, yhalf, zsend, zbuf):
        result = []
        for k, (cond, dx, dy, flip) in enumerate(sources):
            opposite = next(
                j for j, s in enumerate(sources) if s[1] == -dx and s[2] == -dy and s[3] == flip
            )
            if flip:
                src = zsend
                dst = zbuf.at[opposite - 8]
                here = zbuf.at[k - 8]
            else:
                src = face(xfaces, ysend, ysend_half, dx, dy)
                dst = halo(xhalf, ybuf, yhalf, -dx, -dy)
                here = halo(xhalf, ybuf, yhalf, dx, dy)
            target = {"gx": gx + dx, "gy": gy + dy, "col": 1 - col if flip else col}
            out = pltpu.make_async_remote_copy(
                src_ref=src, dst_ref=dst, send_sem=halo_send.at[phase, k],
                recv_sem=halo_recv.at[phase, opposite], device_id=target, device_id_type=MESH_ID,
            )
            arrive = pltpu.make_async_remote_copy(
                src_ref=here, dst_ref=here, send_sem=halo_send.at[phase, k],
                recv_sem=halo_recv.at[phase, k], device_id=target, device_id_type=MESH_ID,
            )
            result.append((cond, out, arrive))
        return result

    def guarded(cond, action):
        if cond is None:
            action()
        else:
            pl.when(cond)(action)

    def zero_absent(xhalf, ybuf, yhalf, zbuf):
        for k, (cond, dx, dy, flip) in enumerate(sources):
            if cond is None:
                continue

            def clear(k=k, dx=dx, dy=dy, flip=flip):
                if flip:
                    zbuf[k - 8] = jnp.zeros(zbuf.shape[1:], zbuf.dtype)
                else:
                    part = halo(xhalf, ybuf, yhalf, dx, dy)
                    part[...] = jnp.zeros(part.shape, part.dtype)

            pl.when(jnp.logical_not(cond))(clear)

    def sum_copies(phase, msg, slots):
        for other in peers:
            pltpu.make_async_remote_copy(
                src_ref=msg, dst_ref=slots.at[me], send_sem=sum_send.at[phase],
                recv_sem=sum_recv.at[phase], device_id=other, device_id_type=MESH_ID,
            ).start()
        slots[me] = msg[...]
        rest = slots.at[pl.ds(0, group - 1)]
        return pltpu.make_async_remote_copy(
            src_ref=rest, dst_ref=rest, send_sem=sum_send.at[phase],
            recv_sem=sum_recv.at[phase], device_id=peers[0], device_id_type=MESH_ID,
        )

    zero_absent(xhalf0, ybuf0, yhalf0, zbuf0)
    zero_absent(xhalf1, ybuf1, yhalf1, zbuf1)

    pl.semaphore_wait(barrier, group - 1)

    pending = []

    def start(copies):
        for cond, out, _ in copies:
            guarded(cond, out.start)
        pending.extend(copies)

    def land(copies):
        for cond, _, arrive in copies:
            guarded(cond, arrive.wait_recv)

    halo0 = exchange(
        0, (warm_s.at[:, 0], warm_s.at[:, cx - 1]), xhalf0,
        ysend0, ysend_half0, ybuf0, yhalf0, zsend0, zbuf0,
    )
    start(halo0)
    total0 = sum_copies(0, msg0, sums0)

    blocks = map_ref.shape
    for bx in range(blocks[0]):
        mus = []
        lms = []
        for by in range(blocks[1]):
            mu = jnp.zeros((8, cz), f32)
            lm = jnp.zeros((8, cz), f32)
            for bz in range(blocks[2]):
                entry = map_ref[bx, by, bz]
                here = (lane[:8] >= 32 * bz) & (lane[:8] < 32 * (bz + 1))
                lm = jnp.where(here, table_ref[0, entry], lm)
                mu = jnp.where(here, table_ref[1, entry], mu)
            mus.append(mu)
            lms.append(lm + mu)
        mu_s[bx] = jnp.concatenate(mus, 0)
        lm_s[bx] = jnp.concatenate(lms, 0)
    xs = lane & (cx - 1)
    mu_edge = jnp.zeros((cy, cz), f32)
    lm_edge = jnp.zeros((cy, cz), f32)
    edge_block = jnp.where(col == 0, blocks[2] - 1, 0)
    for bx in range(blocks[0]):
        for by in range(blocks[1]):
            entry = map_ref[bx, by, edge_block]
            here = ((xs >= 8 * bx) & (xs < 8 * (bx + 1))) & ((row >= 8 * by) & (row < 8 * (by + 1)))
            mu_edge = jnp.where(here, table_ref[1, entry], mu_edge)
            lm_edge = jnp.where(here, table_ref[0, entry] + table_ref[1, entry], lm_edge)

    load_density.wait()

    def prepare(x, carry):
        mu = mu_s[lax.shift_right_logical(x, 3)]
        lm = lm_s[lax.shift_right_logical(x, 3)]
        m = mask_s[x]
        inertia = omega * density_s[x].astype(f32)
        base = 6.0 * mu + 2.0 * lm - inertia
        for c in range(3):
            real = base + m * imp_ref[0, c]
            imag = m * imp_ref[1, c] - DAMPING * inertia
            scale = RELAXATION / (real * real + imag * imag)
            dinv[c, x] = real * scale
            dinv[3 + c, x] = imag * scale
        return carry

    lax.fori_loop(0, cx, prepare, 0, unroll=2)

    def shift_up(v):
        return jnp.where(lane == cz - 1, 0.0, pltpu.roll(v, cz - 1, 1))

    def shift_down(v):
        return jnp.where(lane == 0, 0.0, pltpu.roll(v, 1, 1))

    def z_terms(zbuf):
        sign = jnp.where(col == 0, 0.25, -0.25)
        h, before, after, under, over = (zbuf[k].astype(f32) for k in range(5))
        ahead = jnp.where(xs == cx - 1, pltpu.roll(after, cx - 1, 1), pltpu.roll(h, cz - 1, 1))
        behind = jnp.where(xs == 0, pltpu.roll(before, cz - cx + 1, 1), pltpu.roll(h, 1, 1))
        dxh = (ahead - behind) * sign
        above = jnp.where(row == cy - 1, pltpu.roll(over, cy - 1, 0), pltpu.roll(h, cy - 1, 0))
        below = jnp.where(row == 0, pltpu.roll(under, 1, 0), pltpu.roll(h, 1, 0))
        dyh = (above - below) * sign

        def block(c):
            own = (lane >= c * cx) & (lane < (c + 1) * cx)
            return own | ((lane >= (c + 3) * cx) & (lane < (c + 4) * cx))

        extra = jnp.where(
            block(0),
            pltpu.roll(dxh, cz - 2 * cx, 1),
            jnp.where(
                block(1),
                pltpu.roll(dyh, cz - cx, 1),
                h + pltpu.roll(dxh, 2 * cx, 1) + pltpu.roll(dyh, cx, 1),
            ),
        )
        return mu_edge * h + lm_edge * extra

    def mean_terms(slots):
        total = jnp.sum(slots[...], 0) / jnp.float32(group * cells)
        means = [jnp.sum(jnp.where(lane1 == c, total, 0.0), 1, keepdims=True) for c in range(6)]
        result = []
        for c in range(3):
            result.append(imp_ref[0, c] * means[c] - imp_ref[1, c] * means[3 + c])
        for c in range(3):
            result.append(imp_ref[0, c] * means[3 + c] + imp_ref[1, c] * means[c])
        return [jnp.broadcast_to(r, (1, cz)) for r in result]

    def y_up(v):
        return jnp.where(row == cy - 1, 0.0, pltpu.roll(v, cy - 1, 0))

    def y_down(v):
        return jnp.where(row == 0, 0.0, pltpu.roll(v, 1, 0))

    def halo_slopes(field):
        def step(k, carry):
            px = k * (cx + 1)
            for part in (0, 3):
                uy = field[part + 1, px]
                uz = field[part + 2, px]
                slope_s[part // 3, px] = y_up(uy) - y_down(uy) + (shift_up(uz) - shift_down(uz))
            return carry

        lax.fori_loop(0, 2, step, 0)

    def stencil(field, x):
        px = x + 1
        block_x = lax.shift_right_logical(x, 3)
        mu = mu_s[block_x]
        lm = lm_s[block_x]
        quarter = 0.25 * lm
        for part in (0, 3):
            mid = [field[part + c, px] for c in range(3)]
            xp = [field[part + c, px + 1] for c in range(3)]
            xm = [field[part + c, px - 1] for c in range(3)]
            yp = [y_up(v) for v in mid]
            ym = [y_down(v) for v in mid]
            zp = [shift_up(v) for v in mid]
            zm = [shift_down(v) for v in mid]
            sx = [a + b for a, b in zip(xp, xm)]
            sy = [a + b for a, b in zip(yp, ym)]
            sz = [a + b for a, b in zip(zp, zm)]
            dx0 = xp[0] - xm[0]
            dy1 = yp[1] - ym[1]
            dz2 = zp[2] - zm[2]
            slope_s[part // 3, px] = dy1 + dz2
            by_y = dx0 + dz2
            by_z = dx0 + dy1
            own = [
                lm * sx[0],
                lm * sy[1] + quarter * (y_up(by_y) - y_down(by_y)),
                lm * sz[2] + quarter * (shift_up(by_z) - shift_down(by_z)),
            ]
            for c in range(3):
                s = source_s[part + c, x].astype(f32) + own[c]
                part_s[part + c, x] = s + mu * (sx[c] + sy[c] + sz[c])

    def y_terms(ybuf, yhalf):
        ybuf[:, :, pl.ds(TOP, cx), :] = yhalf[...].astype(f32)
        for side, edge_rows, sign in ((0, pl.ds(0, 8), -0.25), (1, pl.ds(cy - 8, 8), 0.25)):
            mu = jnp.concatenate([mu_s[bx, edge_rows, :] for bx in range(cx // 8)], 0)
            lm = jnp.concatenate([lm_s[bx, edge_rows, :] for bx in range(cx // 8)], 0)
            scaled = lm * sign
            for part in (0, 3):
                h = [ybuf[side, part + c, pl.ds(TOP, cx), :] for c in range(3)]
                dx = [
                    ybuf[side, part + c, pl.ds(TOP + 1, cx), :]
                    - ybuf[side, part + c, pl.ds(TOP - 1, cx), :]
                    for c in range(2)
                ]
                dz = [shift_up(h[c]) - shift_down(h[c]) for c in (1, 2)]
                ky_s[side, part] = mu * h[0] + scaled * dx[1]
                ky_s[side, part + 1] = (mu + lm) * h[1] + scaled * (dx[0] + dz[1])
                ky_s[side, part + 2] = mu * h[2] + scaled * dz[0]

    def finish(field, x, zk, zm):
        px = x + 1
        m = mask_s[x]
        quarter = 0.25 * lm_s[lax.shift_right_logical(x, 3)]
        sums = []
        for c in range(6):
            beyond = pltpu.roll(zk, (edge - (c * cx + x)) & (cz - 1), 1)
            s = part_s[c, x] + jnp.where(lane == edge, beyond, 0.0)
            low = ky_s[0, c, pl.ds(x, 1), :]
            high = ky_s[1, c, pl.ds(x, 1), :]
            s = s + jnp.where(row == 0, low, jnp.where(row == cy - 1, high, 0.0))
            if c % 3 == 0:
                s = s + quarter * (slope_s[c // 3, px + 1] - slope_s[c // 3, px - 1])
            sums.append(s + m * zm[c])
        result = [None] * 6
        for c in range(3):
            dr = dinv[c, x]
            di = dinv[3 + c, x]
            re, im = sums[c], sums[3 + c]
            result[c] = (1.0 - RELAXATION) * field[c, px] + (re * dr + im * di)
            result[3 + c] = (1.0 - RELAXATION) * field[3 + c, px] + (im * dr - re * di)
        return result, m

    def inner(field):
        def step(x, carry):
            stencil(field, x)
            return carry

        lax.fori_loop(1, cx - 1, step, 0, unroll=2)

    def outer(field, xhalf):
        field[:, 0] = xhalf[0].astype(f32)
        field[:, cx + 1] = xhalf[1].astype(f32)

        def step(k, carry):
            stencil(field, k * (cx - 1))
            return carry

        lax.fori_loop(0, 2, step, 0)
        halo_slopes(field)

    load_source.wait()
    inner(f0)
    land(halo0)
    outer(f0, xhalf0)
    y_terms(ybuf0, yhalf0)
    zk0 = z_terms(zbuf0)
    total0.wait_recv()
    zm0 = mean_terms(sums0)

    def sweep_one(x, carry):
        packed, accs = carry
        new, m = finish(f0, x, zk0, zm0)
        grown = []
        for c in range(6):
            f1[c, x + 1] = new[c]
            ysend1[0, c, pl.ds(x, 1), :] = new[c][:1]
            ysend1[1, c, pl.ds(x, 1), :] = new[c][cy - 1 :]
            grown.append(accs[c] + fold(m * new[c]))
            packed = pack(packed, new[c], c, x)
        return packed, tuple(grown)

    def sweep_one_ends(k, carry):
        return sweep_one(k * (cx - 1), carry)

    packed, accs = lax.fori_loop(
        0, 2, sweep_one_ends, (jnp.zeros((cy, cz), f32), zero_acc), unroll=2
    )
    xsend[0] = f1[:, 1].astype(jnp.bfloat16)
    xsend[1] = f1[:, cx].astype(jnp.bfloat16)
    halo1 = exchange(
        1, (xsend.at[0], xsend.at[1]), xhalf1,
        ysend1, ysend_half1, ybuf1, yhalf1, zsend1, zbuf1,
    )
    start(halo1[:2])
    packed, accs = lax.fori_loop(1, cx - 1, sweep_one, (packed, accs), unroll=2)
    zsend1[...] = packed.astype(jnp.bfloat16)
    ysend_half1[...] = ysend1[...].astype(jnp.bfloat16)
    start(halo1[2:])
    msg1[...] = to_row(accs)
    total1 = sum_copies(1, msg1, sums1)

    inner(f1)
    load_forward.wait()
    land(halo1)
    outer(f1, xhalf1)
    y_terms(ybuf1, yhalf1)
    zk1 = z_terms(zbuf1)
    total1.wait_recv()
    zm1 = mean_terms(sums1)

    def sweep_two(x, corr):
        new, _ = finish(f1, x, zk1, zm1)
        for c in range(6):
            out_ref[c, x] = new[c]
        for c in range(3):
            fr = forward_s[c, x].astype(f32)
            fi = forward_s[3 + c, x].astype(f32)
            corr = corr + (new[c] * (fr - DAMPING * fi) - new[3 + c] * (fi + DAMPING * fr))
        return corr

    bands = [
        lax.fori_loop(4 * a, 4 * a + 4, sweep_two, jnp.zeros((cy, cz), f32), unroll=2) for a in range(cx // 4)
    ]
    tall = jnp.concatenate(bands, 0)
    n_rows = tall.shape[0]
    band_sums = jnp.sum(tall, 1, keepdims=True) * (-omega / 64.0)
    spots = lax.broadcasted_iota(jnp.int32, (n_rows, cz), 1) == (
        lax.shift_right_logical(lax.broadcasted_iota(jnp.int32, (n_rows, cz), 0), 2) + gy * (n_rows // 4)
    )
    msg2[...] = jnp.sum(jnp.where(spots, band_sums, 0.0), 0, keepdims=True)
    total2 = sum_copies(2, msg2, sums2)
    per_x, per_y = cx // 4, cy // 4
    assert per_x == 4 and per_y == 4 and cx == 16 and cz == 128 and n_col == 2
    shape = (n_gx * per_x, cz)
    lanes = lax.broadcasted_iota(jnp.int32, shape, 1)
    rows_out = lax.broadcasted_iota(jnp.int32, shape, 0)
    keep = (lax.shift_right_logical(lanes, 2) & (per_x - 1)) == (rows_out & (per_x - 1))
    pick_shape = (n_gy * per_y, cz)
    target = lax.broadcasted_iota(jnp.int32, pick_shape, 0)
    origin = lax.broadcasted_iota(jnp.int32, pick_shape, 1)
    place = lax.shift_right_logical(origin, 4) * per_y + (origin & (per_y - 1))
    pick = jnp.where(place == target, 1.0, 0.0)
    total2.wait_recv()
    wide = jnp.zeros(shape, f32)
    for g in range(n_gx):
        strip = sums2[g * n_gy * n_col]
        for k in range(1, n_gy * n_col):
            strip = strip + sums2[g * n_gy * n_col + k]
        wide = jnp.where((rows_out >= g * per_x) & (rows_out < (g + 1) * per_x), strip, wide)
    wide = jnp.where(keep, wide, 0.0)
    coarse_ref[...] = lax.dot_general(
        pick, wide, (((1,), (1,)), ((), ())),
        preferred_element_type=f32, precision=lax.Precision.HIGHEST,
    )
    for cond, out, _ in pending:
        guarded(cond, out.wait_send)
    for total in (total0, total1, total2):
        total.wait_send()


def shards(n_gx, n_gy, n_col, source, warm, forward, density, material_map, material_table,
           iface_cells, impedance, omega2):
    f32 = jnp.float32
    cx, cy, cz = density.shape
    group = n_gx * n_gy * n_col
    vmem = pl.BlockSpec(memory_space=pltpu.VMEM)
    smem = pl.BlockSpec(memory_space=pltpu.SMEM)
    hbm = pl.BlockSpec(memory_space=pltpu.HBM)
    field = pltpu.VMEM((6, cx + 2, cy, cz), f32)
    tile = (cx, cy, cz)
    y_halo = pltpu.VMEM((2, 6, TOP + cx + 8, cz), f32)
    y_face = pltpu.VMEM((2, 6, cx, cz), f32)
    half = pltpu.VMEM((2, 6, 16, cz), jnp.bfloat16)
    table = material_table.T
    warm, source, density, forward, iface_cells, material_map, table, impedance = (
        pltpu.with_memory_space_constraint(a, pltpu.HBM)
        for a in (warm, source, density, forward, iface_cells, material_map, table, impedance)
    )
    adjoint, coarse = pl.pallas_call(
        functools.partial(kernel, n_gx, n_gy, n_col),
        out_shape=(
            jax.ShapeDtypeStruct((6,) + tile, f32),
            jax.ShapeDtypeStruct((n_gy * (cy // 4), n_gx * (cx // 4)), f32),
        ),
        in_specs=[hbm, hbm, hbm, hbm, vmem, smem, smem, smem, smem],
        out_specs=(vmem, vmem),
        scratch_shapes=[
            field, field,
            pltpu.VMEM((5, cy, cz), jnp.bfloat16), pltpu.VMEM((5, cy, cz), jnp.bfloat16),
            pltpu.VMEM((cy, cz), jnp.bfloat16), pltpu.VMEM((cy, cz), jnp.bfloat16),
            y_halo, y_halo, y_face, y_face,
            half, half, half, half, half, half, half,
            pltpu.VMEM((group, 1, cz), f32), pltpu.VMEM((group, 1, cz), f32),
            pltpu.VMEM((group, 1, cz), f32),
            pltpu.VMEM((1, cz), f32), pltpu.VMEM((1, cz), f32), pltpu.VMEM((1, cz), f32),
            pltpu.VMEM(tile, f32),
            pltpu.VMEM((cx // 8, cy, cz), f32), pltpu.VMEM((cx // 8, cy, cz), f32),
            pltpu.VMEM((6,) + tile, f32),
            pltpu.VMEM((6,) + tile, jnp.bfloat16),
            pltpu.VMEM((6,) + tile, jnp.bfloat16),
            pltpu.VMEM(tile, jnp.bfloat16),
            pltpu.VMEM((6,) + tile, jnp.bfloat16),
            pltpu.VMEM((6,) + tile, f32),
            y_face,
            pltpu.VMEM((2, cx + 2, cy, cz), f32),
            pltpu.SemaphoreType.DMA((4,)),
            pltpu.SemaphoreType.DMA((2, 13)),
            pltpu.SemaphoreType.DMA((2, 13)),
            pltpu.SemaphoreType.DMA((3,)),
            pltpu.SemaphoreType.DMA((3,)),
        ],
        compiler_params=pltpu.CompilerParams(
            collective_id=0, has_side_effects=True, vmem_limit_bytes=32 * 1024 * 1024
        ),
        name="adjoint_sweeps",
    )(warm, source, density, forward, iface_cells, material_map, table, impedance, omega2)
    return adjoint, coarse.T


def solution(mesh):
    in_specs = (
        P("freq", "gx", "gy", "col"),
        P("freq", "gx", "gy", "col"),
        P("freq", "gx", "gy", "col"),
        P("gx", "gy", "col"),
        P("gx", "gy", "col"),
        P(),
        P(("gx", "gy", "col"), None),
        P(),
        P("freq"),
    )
    out_specs = (P("freq", "gx", "gy", "col"), P("freq", None))
    body = functools.partial(shards, mesh.shape["gx"], mesh.shape["gy"], mesh.shape["col"])
    return jax.shard_map(body, mesh=mesh, in_specs=in_specs, out_specs=out_specs, check_vma=False)
```

```python
import functools
import jax
import jax.numpy as jnp
from jax import lax
from jax.experimental import pallas as pl
from jax.experimental.pallas import tpu as pltpu
from jax.sharding import PartitionSpec as P

DAMPING = 0.5
RELAXATION = 0.6
MESH_ID = pl.DeviceIdType.MESH
TOP = 8


def kernel(
    n_gx, n_gy, n_col,
    warm_hbm, source_hbm, density_hbm, forward_hbm, cells_ref,
    map_ref, table_ref, imp_ref, omega_ref,
    out_ref, coarse_ref,
    f0, f1, zbuf0, zbuf1, zsend0, zsend1, ybuf0, ybuf1, ysend0, ysend1,
    xhalf0, xhalf1, xsend, yhalf0, yhalf1, ysend_half0, ysend_half1,
    sums0, sums1, sums2, msg0, msg1, msg2,
    mask_s, mu_s, lm_s, dinv, warm_s, source_s, density_s, forward_s, part_s, ky_s, slope_s,
    local_sem, halo_send, halo_recv, sum_send, sum_recv,
):
    f32 = jnp.float32
    cx, cy, cz = warm_hbm.shape[1:]
    cells = cells_ref.shape[1]
    group = n_gx * n_gy * n_col
    gx = lax.axis_index("gx")
    gy = lax.axis_index("gy")
    col = lax.axis_index("col")
    me = (gx * n_gy + gy) * n_col + col

    def turned(position, length):
        steps = [position + d for d in range(length)]
        return [steps[0]] + [jnp.where(t >= length, t - length, t) for t in steps[1:]]

    peers = []
    for other_gx in turned(gx, n_gx):
        for other_gy in turned(gy, n_gy):
            for other_col in turned(col, n_col):
                peers.append({"gx": other_gx, "gy": other_gy, "col": other_col})
    peers = peers[1:]

    barrier = pltpu.get_barrier_semaphore()
    for other in peers:
        pl.semaphore_signal(barrier, inc=1, device_id=other, device_id_type=MESH_ID)

    load_density = pltpu.make_async_copy(density_hbm, density_s, local_sem.at[0])
    load_source = pltpu.make_async_copy(source_hbm, source_s, local_sem.at[1])
    load_forward = pltpu.make_async_copy(forward_hbm, forward_s, local_sem.at[2])
    load_warm = pltpu.make_async_copy(warm_hbm, warm_s, local_sem.at[3])
    load_warm.start()
    load_density.start()
    load_source.start()
    load_forward.start()

    lane = lax.broadcasted_iota(jnp.int32, (cy, cz), 1)
    row = lax.broadcasted_iota(jnp.int32, (cy, cz), 0)
    lane1 = lax.broadcasted_iota(jnp.int32, (1, cz), 1)
    edge = jnp.where(col == 0, cz - 1, 0)
    omega = omega_ref[0]

    idx = cells_ref[...]
    hot_row = jnp.where(
        lax.broadcasted_iota(jnp.int32, (cx * cy, cells), 0) == lax.shift_right_logical(idx, cz.bit_length() - 1), 1.0, 0.0
    ).astype(jnp.bfloat16)
    hot_lane = jnp.where(
        lax.broadcasted_iota(jnp.int32, (cz, cells), 0) == (idx & (cz - 1)), 1.0, 0.0
    ).astype(jnp.bfloat16)
    mask = lax.dot_general(
        hot_row, hot_lane, (((1,), (1,)), ((), ())), preferred_element_type=f32
    )
    mask_s[...] = mask.reshape(cx, cy, cz)

    def pack(packed, value, c, x):
        spot = c * cx + x
        moved = pltpu.roll(value, (spot - edge) & (cz - 1), 1)
        return jnp.where(lane == spot, moved, packed)

    def fold(value):
        return value[:8] + value[8:]

    def to_row(accs):
        tall = jnp.concatenate([jnp.sum(a, 0, keepdims=True) for a in accs] + [jnp.zeros((2, cz), f32)], 0)
        total = jnp.sum(tall, 1, keepdims=True)
        spots = lax.broadcasted_iota(jnp.int32, (8, cz), 0) == lax.broadcasted_iota(jnp.int32, (8, cz), 1)
        return jnp.sum(jnp.where(spots, total, 0.0), 0, keepdims=True)

    zero_acc = tuple(jnp.zeros((8, cz), f32) for _ in range(6))

    def convert(x, carry):
        packed, accs = carry
        m = mask_s[x]
        grown = []
        for c in range(6):
            v = warm_s[c, x].astype(f32)
            f0[c, x + 1] = v
            ysend0[0, c, pl.ds(x, 1), :] = v[:1]
            ysend0[1, c, pl.ds(x, 1), :] = v[cy - 1 :]
            grown.append(accs[c] + fold(m * v))
            packed = pack(packed, v, c, x)
        return packed, tuple(grown)


    load_warm.wait()
    packed, accs = lax.fori_loop(0, cx, convert, (jnp.zeros((cy, cz), f32), zero_acc), unroll=2)
    zsend0[...] = packed.astype(jnp.bfloat16)
    ysend_half0[...] = ysend0[...].astype(jnp.bfloat16)
    msg0[...] = to_row(accs)

    has = {"xm": gx > 0, "xp": gx < n_gx - 1, "ym": gy > 0, "yp": gy < n_gy - 1}

    def both(a, b):
        return jnp.logical_and(has[a], has[b])

    sources = [
        (has["xm"], -1, 0, False), (has["xp"], 1, 0, False),
        (has["ym"], 0, -1, False), (has["yp"], 0, 1, False),
        (both("xm", "ym"), -1, -1, False), (both("xm", "yp"), -1, 1, False),
        (both("xp", "ym"), 1, -1, False), (both("xp", "yp"), 1, 1, False),
        (None, 0, 0, True),
        (has["xm"], -1, 0, True), (has["xp"], 1, 0, True),
        (has["ym"], 0, -1, True), (has["yp"], 0, 1, True),
    ]

    def face(xfaces, ysend, ysend_half, dx, dy):
        if dy == 0:
            return xfaces[0 if dx < 0 else 1]
        side = 0 if dy < 0 else 1
        if dx == 0:
            return ysend_half.at[side]
        return ysend.at[side, :, pl.ds(0 if dx < 0 else cx - 1, 1), :]

    def halo(xhalf, ybuf, yhalf, dx, dy):
        if dy == 0:
            return xhalf.at[0 if dx < 0 else 1]
        side = 0 if dy < 0 else 1
        if dx == 0:
            return yhalf.at[side]
        return ybuf.at[side, :, pl.ds(TOP - 1 if dx < 0 else TOP + cx, 1), :]

    def exchange(phase, xfaces, xhalf, ysend, ysend_half, ybuf, yhalf, zsend, zbuf):
        result = []
        for k, (cond, dx, dy, flip) in enumerate(sources):
            opposite = next(
                j for j, s in enumerate(sources) if s[1] == -dx and s[2] == -dy and s[3] == flip
            )
            if flip:
                src = zsend
                dst = zbuf.at[opposite - 8]
                here = zbuf.at[k - 8]
            else:
                src = face(xfaces, ysend, ysend_half, dx, dy)
                dst = halo(xhalf, ybuf, yhalf, -dx, -dy)
                here = halo(xhalf, ybuf, yhalf, dx, dy)
            target = {"gx": gx + dx, "gy": gy + dy, "col": 1 - col if flip else col}
            out = pltpu.make_async_remote_copy(
                src_ref=src, dst_ref=dst, send_sem=halo_send.at[phase, k],
                recv_sem=halo_recv.at[phase, opposite], device_id=target, device_id_type=MESH_ID,
            )
            arrive = pltpu.make_async_remote_copy(
                src_ref=here, dst_ref=here, send_sem=halo_send.at[phase, k],
                recv_sem=halo_recv.at[phase, k], device_id=target, device_id_type=MESH_ID,
            )
            result.append((cond, out, arrive))
        return result

    def guarded(cond, action):
        if cond is None:
            action()
        else:
            pl.when(cond)(action)

    def zero_absent(xhalf, ybuf, yhalf, zbuf):
        for k, (cond, dx, dy, flip) in enumerate(sources):
            if cond is None:
                continue

            def clear(k=k, dx=dx, dy=dy, flip=flip):
                if flip:
                    zbuf[k - 8] = jnp.zeros(zbuf.shape[1:], zbuf.dtype)
                else:
                    part = halo(xhalf, ybuf, yhalf, dx, dy)
                    part[...] = jnp.zeros(part.shape, part.dtype)

            pl.when(jnp.logical_not(cond))(clear)

    def sum_copies(phase, msg, slots):
        for other in peers:
            pltpu.make_async_remote_copy(
                src_ref=msg, dst_ref=slots.at[me], send_sem=sum_send.at[phase],
                recv_sem=sum_recv.at[phase], device_id=other, device_id_type=MESH_ID,
            ).start()
        slots[me] = msg[...]
        rest = slots.at[pl.ds(0, group - 1)]
        return pltpu.make_async_remote_copy(
            src_ref=rest, dst_ref=rest, send_sem=sum_send.at[phase],
            recv_sem=sum_recv.at[phase], device_id=peers[0], device_id_type=MESH_ID,
        )

    zero_absent(xhalf0, ybuf0, yhalf0, zbuf0)
    zero_absent(xhalf1, ybuf1, yhalf1, zbuf1)

    pl.semaphore_wait(barrier, group - 1)

    pending = []

    def start(copies):
        for cond, out, _ in copies:
            guarded(cond, out.start)
        pending.extend(copies)

    def land(copies):
        for cond, _, arrive in copies:
            guarded(cond, arrive.wait_recv)

    halo0 = exchange(
        0, (warm_s.at[:, 0], warm_s.at[:, cx - 1]), xhalf0,
        ysend0, ysend_half0, ybuf0, yhalf0, zsend0, zbuf0,
    )
    start(halo0)
    total0 = sum_copies(0, msg0, sums0)

    blocks = map_ref.shape
    for bx in range(blocks[0]):
        mus = []
        lms = []
        for by in range(blocks[1]):
            mu = jnp.zeros((8, cz), f32)
            lm = jnp.zeros((8, cz), f32)
            for bz in range(blocks[2]):
                entry = map_ref[bx, by, bz]
                here = (lane[:8] >= 32 * bz) & (lane[:8] < 32 * (bz + 1))
                lm = jnp.where(here, table_ref[0, entry], lm)
                mu = jnp.where(here, table_ref[1, entry], mu)
            mus.append(mu)
            lms.append(lm + mu)
        mu_s[bx] = jnp.concatenate(mus, 0)
        lm_s[bx] = jnp.concatenate(lms, 0)
    xs = lane & (cx - 1)
    mu_edge = jnp.zeros((cy, cz), f32)
    lm_edge = jnp.zeros((cy, cz), f32)
    edge_block = jnp.where(col == 0, blocks[2] - 1, 0)
    for bx in range(blocks[0]):
        for by in range(blocks[1]):
            entry = map_ref[bx, by, edge_block]
            here = ((xs >= 8 * bx) & (xs < 8 * (bx + 1))) & ((row >= 8 * by) & (row < 8 * (by + 1)))
            mu_edge = jnp.where(here, table_ref[1, entry], mu_edge)
            lm_edge = jnp.where(here, table_ref[0, entry] + table_ref[1, entry], lm_edge)

    load_density.wait()

    def prepare(x, carry):
        mu = mu_s[lax.shift_right_logical(x, 3)]
        lm = lm_s[lax.shift_right_logical(x, 3)]
        m = mask_s[x]
        inertia = omega * density_s[x].astype(f32)
        base = 6.0 * mu + 2.0 * lm - inertia
        for c in range(3):
            real = base + m * imp_ref[0, c]
            imag = m * imp_ref[1, c] - DAMPING * inertia
            scale = RELAXATION / (real * real + imag * imag)
            dinv[c, x] = real * scale
            dinv[3 + c, x] = imag * scale
        return carry

    lax.fori_loop(0, cx, prepare, 0, unroll=2)

    def shift_up(v):
        return jnp.where(lane == cz - 1, 0.0, pltpu.roll(v, cz - 1, 1))

    def shift_down(v):
        return jnp.where(lane == 0, 0.0, pltpu.roll(v, 1, 1))

    def z_terms(zbuf):
        sign = jnp.where(col == 0, 0.25, -0.25)
        h, before, after, under, over = (zbuf[k].astype(f32) for k in range(5))
        ahead = jnp.where(xs == cx - 1, pltpu.roll(after, cx - 1, 1), pltpu.roll(h, cz - 1, 1))
        behind = jnp.where(xs == 0, pltpu.roll(before, cz - cx + 1, 1), pltpu.roll(h, 1, 1))
        dxh = (ahead - behind) * sign
        above = jnp.where(row == cy - 1, pltpu.roll(over, cy - 1, 0), pltpu.roll(h, cy - 1, 0))
        below = jnp.where(row == 0, pltpu.roll(under, 1, 0), pltpu.roll(h, 1, 0))
        dyh = (above - below) * sign

        def block(c):
            own = (lane >= c * cx) & (lane < (c + 1) * cx)
            return own | ((lane >= (c + 3) * cx) & (lane < (c + 4) * cx))

        extra = jnp.where(
            block(0),
            pltpu.roll(dxh, cz - 2 * cx, 1),
            jnp.where(
                block(1),
                pltpu.roll(dyh, cz - cx, 1),
                h + pltpu.roll(dxh, 2 * cx, 1) + pltpu.roll(dyh, cx, 1),
            ),
        )
        return mu_edge * h + lm_edge * extra

    def mean_terms(slots):
        total = jnp.sum(slots[...], 0) / jnp.float32(group * cells)
        means = [jnp.sum(jnp.where(lane1 == c, total, 0.0), 1, keepdims=True) for c in range(6)]
        result = []
        for c in range(3):
            result.append(imp_ref[0, c] * means[c] - imp_ref[1, c] * means[3 + c])
        for c in range(3):
            result.append(imp_ref[0, c] * means[3 + c] + imp_ref[1, c] * means[c])
        return [jnp.broadcast_to(r, (1, cz)) for r in result]

    def y_up(v):
        return jnp.where(row == cy - 1, 0.0, pltpu.roll(v, cy - 1, 0))

    def y_down(v):
        return jnp.where(row == 0, 0.0, pltpu.roll(v, 1, 0))

    def halo_slopes(field):
        def step(k, carry):
            px = k * (cx + 1)
            for part in (0, 3):
                uy = field[part + 1, px]
                uz = field[part + 2, px]
                slope_s[part // 3, px] = y_up(uy) - y_down(uy) + (shift_up(uz) - shift_down(uz))
            return carry

        lax.fori_loop(0, 2, step, 0, unroll=2)

    def stencil(field, x):
        px = x + 1
        block_x = lax.shift_right_logical(x, 3)
        mu = mu_s[block_x]
        lm = lm_s[block_x]
        quarter = 0.25 * lm
        for part in (0, 3):
            mid = [field[part + c, px] for c in range(3)]
            xp = [field[part + c, px + 1] for c in range(3)]
            xm = [field[part + c, px - 1] for c in range(3)]
            yp = [y_up(v) for v in mid]
            ym = [y_down(v) for v in mid]
            zp = [shift_up(v) for v in mid]
            zm = [shift_down(v) for v in mid]
            sx = [a + b for a, b in zip(xp, xm)]
            sy = [a + b for a, b in zip(yp, ym)]
            sz = [a + b for a, b in zip(zp, zm)]
            dx0 = xp[0] - xm[0]
            dy1 = yp[1] - ym[1]
            dz2 = zp[2] - zm[2]
            slope_s[part // 3, px] = dy1 + dz2
            by_y = dx0 + dz2
            by_z = dx0 + dy1
            own = [
                lm * sx[0],
                lm * sy[1] + quarter * (y_up(by_y) - y_down(by_y)),
                lm * sz[2] + quarter * (shift_up(by_z) - shift_down(by_z)),
            ]
            for c in range(3):
                s = source_s[part + c, x].astype(f32) + own[c]
                part_s[part + c, x] = s + mu * (sx[c] + sy[c] + sz[c])

    def y_terms(ybuf, yhalf):
        ybuf[:, :, pl.ds(TOP, cx), :] = yhalf[...].astype(f32)
        for side, edge_rows, sign in ((0, pl.ds(0, 8), -0.25), (1, pl.ds(cy - 8, 8), 0.25)):
            mu = jnp.concatenate([mu_s[bx, edge_rows, :] for bx in range(cx // 8)], 0)
            lm = jnp.concatenate([lm_s[bx, edge_rows, :] for bx in range(cx // 8)], 0)
            scaled = lm * sign
            for part in (0, 3):
                h = [ybuf[side, part + c, pl.ds(TOP, cx), :] for c in range(3)]
                dx = [
                    ybuf[side, part + c, pl.ds(TOP + 1, cx), :]
                    - ybuf[side, part + c, pl.ds(TOP - 1, cx), :]
                    for c in range(2)
                ]
                dz = [shift_up(h[c]) - shift_down(h[c]) for c in (1, 2)]
                ky_s[side, part] = mu * h[0] + scaled * dx[1]
                ky_s[side, part + 1] = (mu + lm) * h[1] + scaled * (dx[0] + dz[1])
                ky_s[side, part + 2] = mu * h[2] + scaled * dz[0]

    def finish(field, x, zk, zm):
        px = x + 1
        m = mask_s[x]
        quarter = 0.25 * lm_s[lax.shift_right_logical(x, 3)]
        sums = []
        for c in range(6):
            beyond = pltpu.roll(zk, (edge - (c * cx + x)) & (cz - 1), 1)
            s = part_s[c, x] + jnp.where(lane == edge, beyond, 0.0)
            low = ky_s[0, c, pl.ds(x, 1), :]
            high = ky_s[1, c, pl.ds(x, 1), :]
            s = s + jnp.where(row == 0, low, jnp.where(row == cy - 1, high, 0.0))
            if c % 3 == 0:
                s = s + quarter * (slope_s[c // 3, px + 1] - slope_s[c // 3, px - 1])
            sums.append(s + m * zm[c])
        result = [None] * 6
        for c in range(3):
            dr = dinv[c, x]
            di = dinv[3 + c, x]
            re, im = sums[c], sums[3 + c]
            result[c] = (1.0 - RELAXATION) * field[c, px] + (re * dr + im * di)
            result[3 + c] = (1.0 - RELAXATION) * field[3 + c, px] + (im * dr - re * di)
        return result, m

    def inner(field):
        def step(x, carry):
            stencil(field, x)
            return carry

        lax.fori_loop(1, cx - 1, step, 0, unroll=2)

    def outer(field, xhalf):
        field[:, 0] = xhalf[0].astype(f32)
        field[:, cx + 1] = xhalf[1].astype(f32)

        def step(k, carry):
            stencil(field, k * (cx - 1))
            return carry

        lax.fori_loop(0, 2, step, 0, unroll=2)
        halo_slopes(field)

    load_source.wait()
    inner(f0)
    land(halo0[:2])
    outer(f0, xhalf0)
    land(halo0[2:])
    y_terms(ybuf0, yhalf0)
    zk0 = z_terms(zbuf0)
    total0.wait_recv()
    zm0 = mean_terms(sums0)

    def sweep_one(x, carry):
        packed, accs = carry
        new, m = finish(f0, x, zk0, zm0)
        grown = []
        for c in range(6):
            f1[c, x + 1] = new[c]
            ysend1[0, c, pl.ds(x, 1), :] = new[c][:1]
            ysend1[1, c, pl.ds(x, 1), :] = new[c][cy - 1 :]
            grown.append(accs[c] + fold(m * new[c]))
            packed = pack(packed, new[c], c, x)
        return packed, tuple(grown)

    def sweep_one_ends(k, carry):
        return sweep_one(k * (cx - 1), carry)

    packed, accs = lax.fori_loop(
        0, 2, sweep_one_ends, (jnp.zeros((cy, cz), f32), zero_acc), unroll=2
    )
    xsend[0] = f1[:, 1].astype(jnp.bfloat16)
    xsend[1] = f1[:, cx].astype(jnp.bfloat16)
    halo1 = exchange(
        1, (xsend.at[0], xsend.at[1]), xhalf1,
        ysend1, ysend_half1, ybuf1, yhalf1, zsend1, zbuf1,
    )
    start(halo1[:2])
    packed, accs = lax.fori_loop(1, cx - 1, sweep_one, (packed, accs), unroll=2)
    zsend1[...] = packed.astype(jnp.bfloat16)
    ysend_half1[...] = ysend1[...].astype(jnp.bfloat16)
    start(halo1[2:])
    msg1[...] = to_row(accs)
    total1 = sum_copies(1, msg1, sums1)

    inner(f1)
    load_forward.wait()
    land(halo1[:2])
    outer(f1, xhalf1)
    land(halo1[2:])
    y_terms(ybuf1, yhalf1)
    zk1 = z_terms(zbuf1)
    total1.wait_recv()
    zm1 = mean_terms(sums1)

    def sweep_two(x, corr):
        new, _ = finish(f1, x, zk1, zm1)
        for c in range(6):
            out_ref[c, x] = new[c]
        for c in range(3):
            fr = forward_s[c, x].astype(f32)
            fi = forward_s[3 + c, x].astype(f32)
            corr = corr + (new[c] * (fr - DAMPING * fi) - new[3 + c] * (fi + DAMPING * fr))
        return corr

    bands = [
        lax.fori_loop(4 * a, 4 * a + 4, sweep_two, jnp.zeros((cy, cz), f32), unroll=2) for a in range(cx // 4)
    ]
    tall = jnp.concatenate(bands, 0)
    n_rows = tall.shape[0]
    band_sums = jnp.sum(tall, 1, keepdims=True) * (-omega / 64.0)
    spots = lax.broadcasted_iota(jnp.int32, (n_rows, cz), 1) == (
        lax.shift_right_logical(lax.broadcasted_iota(jnp.int32, (n_rows, cz), 0), 2) + gy * (n_rows // 4)
    )
    msg2[...] = jnp.sum(jnp.where(spots, band_sums, 0.0), 0, keepdims=True)
    total2 = sum_copies(2, msg2, sums2)
    per_x, per_y = cx // 4, cy // 4
    assert per_x == 4 and per_y == 4 and cx == 16 and cz == 128 and n_col == 2
    shape = (n_gx * per_x, cz)
    lanes = lax.broadcasted_iota(jnp.int32, shape, 1)
    rows_out = lax.broadcasted_iota(jnp.int32, shape, 0)
    keep = (lax.shift_right_logical(lanes, 2) & (per_x - 1)) == (rows_out & (per_x - 1))
    pick_shape = (n_gy * per_y, cz)
    target = lax.broadcasted_iota(jnp.int32, pick_shape, 0)
    origin = lax.broadcasted_iota(jnp.int32, pick_shape, 1)
    place = lax.shift_right_logical(origin, 4) * per_y + (origin & (per_y - 1))
    pick = jnp.where(place == target, 1.0, 0.0)
    total2.wait_recv()
    wide = jnp.zeros(shape, f32)
    for g in range(n_gx):
        strip = sums2[g * n_gy * n_col]
        for k in range(1, n_gy * n_col):
            strip = strip + sums2[g * n_gy * n_col + k]
        wide = jnp.where((rows_out >= g * per_x) & (rows_out < (g + 1) * per_x), strip, wide)
    wide = jnp.where(keep, wide, 0.0)
    coarse_ref[...] = lax.dot_general(
        pick, wide, (((1,), (1,)), ((), ())),
        preferred_element_type=f32, precision=lax.Precision.HIGHEST,
    )
    for cond, out, _ in pending:
        guarded(cond, out.wait_send)
    for total in (total0, total1, total2):
        total.wait_send()


def shards(n_gx, n_gy, n_col, source, warm, forward, density, material_map, material_table,
           iface_cells, impedance, omega2):
    f32 = jnp.float32
    cx, cy, cz = density.shape
    group = n_gx * n_gy * n_col
    vmem = pl.BlockSpec(memory_space=pltpu.VMEM)
    smem = pl.BlockSpec(memory_space=pltpu.SMEM)
    hbm = pl.BlockSpec(memory_space=pltpu.HBM)
    field = pltpu.VMEM((6, cx + 2, cy, cz), f32)
    tile = (cx, cy, cz)
    y_halo = pltpu.VMEM((2, 6, TOP + cx + 8, cz), f32)
    y_face = pltpu.VMEM((2, 6, cx, cz), f32)
    half = pltpu.VMEM((2, 6, 16, cz), jnp.bfloat16)
    table = material_table.T
    warm, source, density, forward, iface_cells, material_map, table, impedance = (
        pltpu.with_memory_space_constraint(a, pltpu.HBM)
        for a in (warm, source, density, forward, iface_cells, material_map, table, impedance)
    )
    adjoint, coarse = pl.pallas_call(
        functools.partial(kernel, n_gx, n_gy, n_col),
        out_shape=(
            jax.ShapeDtypeStruct((6,) + tile, f32),
            jax.ShapeDtypeStruct((n_gy * (cy // 4), n_gx * (cx // 4)), f32),
        ),
        in_specs=[hbm, hbm, hbm, hbm, vmem, smem, smem, smem, smem],
        out_specs=(vmem, vmem),
        scratch_shapes=[
            field, field,
            pltpu.VMEM((5, cy, cz), jnp.bfloat16), pltpu.VMEM((5, cy, cz), jnp.bfloat16),
            pltpu.VMEM((cy, cz), jnp.bfloat16), pltpu.VMEM((cy, cz), jnp.bfloat16),
            y_halo, y_halo, y_face, y_face,
            half, half, half, half, half, half, half,
            pltpu.VMEM((group, 1, cz), f32), pltpu.VMEM((group, 1, cz), f32),
            pltpu.VMEM((group, 1, cz), f32),
            pltpu.VMEM((1, cz), f32), pltpu.VMEM((1, cz), f32), pltpu.VMEM((1, cz), f32),
            pltpu.VMEM(tile, f32),
            pltpu.VMEM((cx // 8, cy, cz), f32), pltpu.VMEM((cx // 8, cy, cz), f32),
            pltpu.VMEM((6,) + tile, f32),
            pltpu.VMEM((6,) + tile, jnp.bfloat16),
            pltpu.VMEM((6,) + tile, jnp.bfloat16),
            pltpu.VMEM(tile, jnp.bfloat16),
            pltpu.VMEM((6,) + tile, jnp.bfloat16),
            pltpu.VMEM((6,) + tile, f32),
            y_face,
            pltpu.VMEM((2, cx + 2, cy, cz), f32),
            pltpu.SemaphoreType.DMA((4,)),
            pltpu.SemaphoreType.DMA((2, 13)),
            pltpu.SemaphoreType.DMA((2, 13)),
            pltpu.SemaphoreType.DMA((3,)),
            pltpu.SemaphoreType.DMA((3,)),
        ],
        compiler_params=pltpu.CompilerParams(
            collective_id=0, has_side_effects=True, vmem_limit_bytes=32 * 1024 * 1024
        ),
        name="adjoint_sweeps",
    )(warm, source, density, forward, iface_cells, material_map, table, impedance, omega2)
    return adjoint, coarse.T


def solution(mesh):
    in_specs = (
        P("freq", "gx", "gy", "col"),
        P("freq", "gx", "gy", "col"),
        P("freq", "gx", "gy", "col"),
        P("gx", "gy", "col"),
        P("gx", "gy", "col"),
        P(),
        P(("gx", "gy", "col"), None),
        P(),
        P("freq"),
    )
    out_specs = (P("freq", "gx", "gy", "col"), P("freq", None))
    body = functools.partial(shards, mesh.shape["gx"], mesh.shape["gy"], mesh.shape["col"])
    return jax.shard_map(body, mesh=mesh, in_specs=in_specs, out_specs=out_specs, check_vma=False)
```
